32 devices in a mesh: replica: 2 (over y), adapter: 16 (over z, x, core).
Axes of the slice: x: 2, y: 2, z: 4, core: 2. Of those that a mesh axis runs over, the one named last changes fastest.
Arguments:
- hidden: bfloat16 [2, 32, 8192], P(None, ('replica', 'adapter')), parts along dimension 1, may hold values from -6 to 6
- input_norm_gain: float32 [8192], replicated, may hold values from 0.5 to 1.5
- query_weight: bfloat16 [8192, 8192], P(None, 'adapter'), may hold values from -0.0625 to 0.0625
- key_value_weight: bfloat16 [8192, 2048], P(None, 'adapter'), may hold values from -0.0625 to 0.0625
- adapter_down_weight: bfloat16 [32, 64, 8192], P(('replica', 'adapter')), parts along dimension 0, may hold values from -0.0625 to 0.0625
- adapter_up_weight: bfloat16 [32, 64, 8192], P('replica', None, 'adapter'), parts along dimension 0, may hold values from -0.75 to 0.75
- key_value_cache: bfloat16 [32, 2, 512, 1024], P(('replica', 'adapter')), parts along dimension 0, may hold values from -110 to 110
- valid_cache_lengths: int32 [32], P(('replica', 'adapter')), parts along dimension 0, may hold values from 4 to 512, as said below
- request_per_slot: int32 [32, 2], P('replica'), parts along dimension 0, may hold values from 0 to 16, as said below
- slot_per_request: int32 [32], P('replica'), parts along dimension 0, may hold values from 0 to 31, as said below
Outputs:
- attended: bfloat16 [2, 32, 8192], P(None, ('replica', 'adapter')), parts along dimension 1
The draws below stay inside these ranges and needn't reach their ends.
There are 2 independent parts, one for each index of `replica`. The reference program is written for one: setup_inputs(seed, part) draws one part's arguments, and reference() takes and returns one part's arrays. A program takes and returns all parts, laid end to end along the dimension named above; an argument that names none is the same for every part. Nothing has to cross between parts.
Inputs may be any that keep to these rules, and one draw needn't show every extreme that they name: `request_per_slot`: each entry is a request index, or 16 for an empty slot; every request stands in exactly one slot; in every draw some adapter has all 2 slots filled, and some slot is empty. request_per_slot at slot slot_per_request[r] (row slot_per_request[r] // 2, column slot_per_request[r] % 2) is r; the last slot of the last adapter is always used. `valid_cache_lengths`: some request's cache is full (512) in every draw.
All inputs are finite; a program needn't handle non-finite values.
Results may differ from the reference program's by a relative error of at most 0.012.
The reference program's roundings to bfloat16 on the way count: a program that leaves them out, or rounds other values in their place, can miss the bound.
Values may be sent and summed in bfloat16 or wider, within the bound.
A program may use at most 64 MiB of HBM per device.

```python
import jax
import jax.numpy as jnp
from jax import lax

MODEL_WIDTH = 8192
QUERY_HEADS = 64
KEY_VALUE_HEADS = 8
HEAD_SIZE = 128
ADAPTER_RANK = 64
DEVICE_REQUESTS = 1
CACHE_CAPACITY = 512
ADAPTER_SLOTS = 2
REQUEST_COUNT = 16
ADAPTER_COUNT = 16
QUERY_FEATURES = 8192
KVW = 2048


def route_draw(key):
    key_base, key_heat, key_hot, key_perm = jax.random.split(jax.random.fold_in(key, 11), 4)
    base_score = jax.random.randint(key_base, (ADAPTER_COUNT, ADAPTER_SLOTS), 0, 2 ** 20)
    heat_level = jax.random.randint(key_heat, (ADAPTER_COUNT, 1), 0, 2 ** 17)
    hot_adapter = jax.random.randint(key_hot, (), 0, ADAPTER_COUNT)
    score = base_score + jnp.arange(ADAPTER_SLOTS, dtype=jnp.int32)[None, :] * heat_level
    score = jnp.where(jnp.arange(ADAPTER_COUNT, dtype=jnp.int32)[:, None] == hot_adapter, -1, score).reshape(-1)
    score = jnp.where(jnp.arange(ADAPTER_COUNT * ADAPTER_SLOTS, dtype=jnp.int32) == ADAPTER_COUNT * ADAPTER_SLOTS - 1, -1, score)
    order = jnp.argsort(score, stable=True).astype(jnp.int32)
    chosen = order[:REQUEST_COUNT]
    shuffle = jax.random.permutation(key_perm, REQUEST_COUNT)
    slot_of_request = chosen[shuffle].astype(jnp.int32)
    table = jnp.full((ADAPTER_COUNT * ADAPTER_SLOTS,), REQUEST_COUNT, jnp.int32).at[slot_of_request].set(jnp.arange(REQUEST_COUNT, dtype=jnp.int32))
    return (table.reshape(ADAPTER_COUNT, ADAPTER_SLOTS), slot_of_request)


def draw_request_per_slot(key, part):
    return route_draw(key)[0]


def draw_slot_per_request(key, part):
    return route_draw(key)[1]


def draw_valid_cache_lengths(key, part):
    key = jax.random.fold_in(key, 7)
    key_len, key_pick = jax.random.split(key)
    lengths = jax.random.randint(key_len, (REQUEST_COUNT,), 4, CACHE_CAPACITY + 1)
    selected_rows = jax.random.randint(key_pick, (), 0, REQUEST_COUNT)
    return jnp.where(jnp.arange(REQUEST_COUNT, dtype=jnp.int32) == selected_rows, CACHE_CAPACITY, lengths).astype(jnp.int32)


def draw_key_value_cache(key, part):
    key = jax.random.fold_in(key, 5)
    key_body = jax.random.fold_in(key, 0)
    array_shape = (REQUEST_COUNT, 2, CACHE_CAPACITY, KEY_VALUE_HEADS * HEAD_SIZE)
    cache = jnp.clip(jax.random.normal(key_body, array_shape, jnp.float32), -6.0, 6.0)
    return cache.astype(jnp.bfloat16)


def block_scale(own_key, extent, pieces, low, high):
    factor_of = 1.0
    for dim, parts in pieces:
        heights = jax.random.uniform(jax.random.fold_in(jax.random.fold_in(own_key, 6), dim), (parts,), jnp.float32, low / len(pieces), high / len(pieces))
        factor_of = factor_of * jnp.repeat(jnp.exp(heights), extent[dim] // parts).reshape((-1,) + (1,) * (len(extent) - 1 - dim))
    return factor_of


def bell_draw(own_key, dims, scale, most, pieces=(), held_as=jnp.bfloat16):
    array = scale * jax.random.normal(own_key, dims, jnp.float32)
    if pieces:
        array = array * block_scale(own_key, dims, pieces, -0.22, 0.18)
    return jnp.clip(array, -most, most).astype(held_as)


def setup_inputs(seed: int = 0, part: int = 0) -> dict:
    key_of = jax.random.split(jax.random.key(seed), 11)
    part_splits = jax.random.split(jax.random.fold_in(key_of[10], part), 11)
    hidden = bell_draw(part_splits[0], (2, REQUEST_COUNT, MODEL_WIDTH), 1.0, 6.0, ((1, 16),))
    input_norm_gain = jnp.clip(1.0 + 0.1 * jax.random.normal(key_of[1], (MODEL_WIDTH,), jnp.float32), 0.5, 1.5)
    query_weight = bell_draw(key_of[2], (MODEL_WIDTH, QUERY_FEATURES), MODEL_WIDTH ** -0.5, 0.0625, ((1, 16),))
    key_value_weight = bell_draw(key_of[3], (MODEL_WIDTH, KVW), MODEL_WIDTH ** -0.5, 0.0625, ((1, 16),))
    adapter_down_weight = bell_draw(part_splits[4], (ADAPTER_COUNT, ADAPTER_RANK, MODEL_WIDTH), MODEL_WIDTH ** -0.5, 0.0625, ((0, 16),))
    adapter_up_weight = bell_draw(part_splits[5], (ADAPTER_COUNT, ADAPTER_RANK, QUERY_FEATURES), ADAPTER_RANK ** -0.5, 0.75, ((2, 16),))
    key_value_cache = draw_key_value_cache(jax.random.fold_in(jax.random.fold_in(key_of[10], part), 71), part)
    valid_cache_lengths = draw_valid_cache_lengths(jax.random.fold_in(jax.random.fold_in(key_of[10], part), 71), part)
    request_per_slot = draw_request_per_slot(jax.random.fold_in(jax.random.fold_in(key_of[10], part), 71), part)
    slot_per_request = draw_slot_per_request(jax.random.fold_in(jax.random.fold_in(key_of[10], part), 71), part)
    return dict(hidden=hidden, input_norm_gain=input_norm_gain, query_weight=query_weight, key_value_weight=key_value_weight, adapter_down_weight=adapter_down_weight, adapter_up_weight=adapter_up_weight, key_value_cache=key_value_cache, valid_cache_lengths=valid_cache_lengths, request_per_slot=request_per_slot, slot_per_request=slot_per_request)


ADAPTER_SCALE = 0.5
ROPE_BASE = 500000.0

def rms_norm(hidden_rows, input_norm_gain):
    values = hidden_rows.astype(jnp.float32)
    spread = lax.optimization_barrier(jnp.mean(values * values, axis=-1, keepdims=True))
    return (values * lax.rsqrt(spread + 1e-05) * input_norm_gain.astype(jnp.float32)).astype(jnp.bfloat16)

def apply_rotation(values, token_positions, heads):
    batch_row_list = values.shape[0]
    shaped = values.reshape(batch_row_list, heads, -1)
    half_dim = shaped.shape[-1] // 2
    frequency = ROPE_BASE ** (-jnp.arange(half_dim, dtype=jnp.float32) / half_dim)
    angles = token_positions.astype(jnp.float32)[:, None, None] * frequency[None, None, :]
    cosine = jnp.cos(angles)
    sine_part = jnp.sin(angles)
    first = shaped[..., :half_dim]
    second = shaped[..., half_dim:]
    turned = jnp.concatenate([first * cosine - second * sine_part, second * cosine + first * sine_part], axis=-1)
    return turned.reshape(batch_row_list, -1)

def attend(query_row_list, block_of_cache, lengths, latest_keys, latest_values):
    batch_row_list = query_row_list.shape[0]
    query_matrix = query_row_list.reshape(batch_row_list, KEY_VALUE_HEADS, QUERY_HEADS // KEY_VALUE_HEADS, HEAD_SIZE).astype(jnp.float32)
    cached_key_rows = block_of_cache[:, 0].reshape(batch_row_list, -1, KEY_VALUE_HEADS, HEAD_SIZE).astype(jnp.float32)
    cached_value_rows = block_of_cache[:, 1].reshape(batch_row_list, -1, KEY_VALUE_HEADS, HEAD_SIZE).astype(jnp.float32)
    appended_keys = latest_keys.reshape(batch_row_list, -1, KEY_VALUE_HEADS, HEAD_SIZE).astype(jnp.float32)
    appended_values = latest_values.reshape(batch_row_list, -1, KEY_VALUE_HEADS, HEAD_SIZE).astype(jnp.float32)
    score_scale = HEAD_SIZE ** (-0.5)
    old_scores = jnp.einsum('bhgd,blhd->bhgl', query_matrix, cached_key_rows) * score_scale
    valid_mask = (jnp.arange(cached_key_rows.shape[1])[None, :] < lengths[:, None])[:, None, None, :]
    old_scores = jnp.where(valid_mask, old_scores, -1e+30)
    new_scores = jnp.einsum('bhgd,bshd->bhgs', query_matrix, appended_keys) * score_scale
    row_top = jnp.maximum(lax.optimization_barrier(jnp.max(old_scores, axis=-1)), lax.optimization_barrier(jnp.max(new_scores, axis=-1)))[..., None]
    old_weights = jnp.where(valid_mask, jnp.exp(old_scores - row_top), 0.0)
    new_weights = jnp.exp(new_scores - row_top)
    weight_total = lax.optimization_barrier(jnp.sum(old_weights, axis=-1, keepdims=True)) + lax.optimization_barrier(jnp.sum(new_weights, axis=-1, keepdims=True))
    old_probs = (old_weights / weight_total).astype(jnp.bfloat16).astype(jnp.float32)
    new_probs = (new_weights / weight_total).astype(jnp.bfloat16).astype(jnp.float32)
    mixed = jnp.einsum('bhgl,blhd->bhgd', old_probs, cached_value_rows) + jnp.einsum('bhgs,bshd->bhgd', new_probs, appended_values)
    return mixed.reshape(batch_row_list, -1).astype(jnp.bfloat16)

def reference(hidden, input_norm_gain, query_weight, key_value_weight, adapter_down_weight, adapter_up_weight, key_value_cache, valid_cache_lengths, request_per_slot, slot_per_request):
    results = []
    fresh_keys_list = []
    latest_value_list = []
    block_list = REQUEST_COUNT // DEVICE_REQUESTS
    for step_index in range(2):
        normed = rms_norm(hidden[step_index], input_norm_gain)
        base_query = jnp.dot(normed, query_weight, preferred_element_type=jnp.float32)
        base_kv = jnp.dot(normed, key_value_weight, preferred_element_type=jnp.float32)
        padded = jnp.concatenate([normed, jnp.zeros((1, MODEL_WIDTH), jnp.bfloat16)], axis=0)

        def shrink_single(pair):
            indices, down_matrix = pair
            return jnp.dot(padded[indices], down_matrix.T, preferred_element_type=jnp.float32).astype(jnp.bfloat16)
        reduced_rows = lax.map(shrink_single, (request_per_slot, adapter_down_weight))

        def expand_single(pair):
            rank_rows, up_matrix = pair
            return jnp.dot(rank_rows, up_matrix, preferred_element_type=jnp.float32)
        adapter_delta = lax.map(expand_single, (reduced_rows, adapter_up_weight)).reshape(ADAPTER_COUNT * ADAPTER_SLOTS, QUERY_FEATURES)[slot_per_request]
        query_vector = (base_query + ADAPTER_SCALE * adapter_delta).astype(jnp.bfloat16)
        key_value_pair = base_kv.astype(jnp.bfloat16)
        token_positions = valid_cache_lengths + step_index
        rotated_query = apply_rotation(query_vector.astype(jnp.float32), token_positions, QUERY_HEADS).astype(jnp.bfloat16)
        incoming_key = apply_rotation(key_value_pair[:, :KEY_VALUE_HEADS * HEAD_SIZE].astype(jnp.float32), token_positions, KEY_VALUE_HEADS).astype(jnp.bfloat16)
        fresh_keys_list.append(incoming_key)
        latest_value_list.append(key_value_pair[:, KEY_VALUE_HEADS * HEAD_SIZE:])
        latest_keys = jnp.stack(fresh_keys_list, axis=1)
        latest_values = jnp.stack(latest_value_list, axis=1)
        current_steps = latest_keys.shape[1]

        def block_attention(block):
            return attend(*block)
        block_output = lax.map(block_attention, (rotated_query.reshape(block_list, DEVICE_REQUESTS, QUERY_FEATURES), key_value_cache.reshape(block_list, DEVICE_REQUESTS, 2, CACHE_CAPACITY, KEY_VALUE_HEADS * HEAD_SIZE), valid_cache_lengths.reshape(block_list, DEVICE_REQUESTS), latest_keys.reshape(block_list, DEVICE_REQUESTS, current_steps, KEY_VALUE_HEADS * HEAD_SIZE), latest_values.reshape(block_list, DEVICE_REQUESTS, current_steps, KEY_VALUE_HEADS * HEAD_SIZE)))
        results.append(block_output.reshape(REQUEST_COUNT, QUERY_FEATURES))
    return jnp.stack(results)
```

```python
import functools
import math

import jax
import jax.numpy as jnp
from jax import lax
from jax.experimental import pallas as pl
from jax.experimental.pallas import tpu as pltpu
from jax.sharding import PartitionSpec as P

QUERY_HEADS = 64
KEY_VALUE_HEADS = 8
HEAD_SIZE = 128
ADP_DEV = 1
ADAPTER_RANK = 64


ADAPTER_SCALE = 0.5
ROPE_BASE = 500000.0


def rms_norm(hidden_rows, input_norm_gain):
    values = hidden_rows.astype(jnp.float32)
    spread = jnp.mean(values * values, axis=-1, keepdims=True)
    return (values * lax.rsqrt(spread + 1e-05) * input_norm_gain).astype(jnp.bfloat16)


def apply_rotation(values, token_positions, heads):
    batch_row_list = values.shape[0]
    shaped = values.reshape(batch_row_list, heads, -1)
    half_dim = shaped.shape[-1] // 2
    frequency = ROPE_BASE ** (-jnp.arange(half_dim, dtype=jnp.float32) / half_dim)
    angles = token_positions.astype(jnp.float32)[:, None, None] * frequency[None, None, :]
    cosine = jnp.cos(angles)
    sine_part = jnp.sin(angles)
    first = shaped[..., :half_dim]
    second = shaped[..., half_dim:]
    turned = jnp.concatenate(
        [first * cosine - second * sine_part, second * cosine + first * sine_part], axis=-1
    )
    return turned.reshape(batch_row_list, -1)


def attend(query_row_list, block_of_cache, lengths, latest_keys, latest_values):
    batch_row_list = query_row_list.shape[0]
    query_matrix = query_row_list.reshape(
        batch_row_list, KEY_VALUE_HEADS, QUERY_HEADS // KEY_VALUE_HEADS, HEAD_SIZE
    )
    cached_key_rows = block_of_cache[:, 0].reshape(batch_row_list, -1, KEY_VALUE_HEADS, HEAD_SIZE)
    cached_value_rows = block_of_cache[:, 1].reshape(batch_row_list, -1, KEY_VALUE_HEADS, HEAD_SIZE)
    appended_keys = latest_keys.reshape(batch_row_list, -1, KEY_VALUE_HEADS, HEAD_SIZE)
    appended_values = latest_values.reshape(batch_row_list, -1, KEY_VALUE_HEADS, HEAD_SIZE)
    score_scale = HEAD_SIZE ** (-0.5)
    old_scores = (
        jnp.einsum(
            "bhgd,blhd->bhgl", query_matrix, cached_key_rows, preferred_element_type=jnp.float32
        )
        * score_scale
    )
    valid_mask = (jnp.arange(cached_key_rows.shape[1])[None, :] < lengths[:, None])[
        :, None, None, :
    ]
    old_scores = jnp.where(valid_mask, old_scores, -1e30)
    new_scores = (
        jnp.einsum(
            "bhgd,bshd->bhgs", query_matrix, appended_keys, preferred_element_type=jnp.float32
        )
        * score_scale
    )
    row_top = jnp.maximum(jnp.max(old_scores, axis=-1), jnp.max(new_scores, axis=-1))[..., None]
    old_weights = jnp.where(valid_mask, jnp.exp(old_scores - row_top), 0.0)
    new_weights = jnp.exp(new_scores - row_top)
    weight_total = jnp.sum(old_weights, axis=-1, keepdims=True) + jnp.sum(
        new_weights, axis=-1, keepdims=True
    )
    old_probs = (old_weights / weight_total).astype(jnp.bfloat16)
    new_probs = (new_weights / weight_total).astype(jnp.bfloat16)
    mixed = jnp.einsum(
        "bhgl,blhd->bhgd", old_probs, cached_value_rows, preferred_element_type=jnp.float32
    )
    mixed = mixed + jnp.einsum(
        "bhgs,bshd->bhgd", new_probs, appended_values, preferred_element_type=jnp.float32
    )
    return mixed.reshape(batch_row_list, -1).astype(jnp.bfloat16)


def project_input(
    block_of_rows,
    query_weight,
    key_value_weight,
    adapter_down_weight,
    adapter_up_weight,
    device_slots,
    slot_per_request,
):
    base_query = jnp.dot(block_of_rows, query_weight, preferred_element_type=jnp.float32)
    base_kv = jnp.dot(block_of_rows, key_value_weight, preferred_element_type=jnp.float32)
    padded = jnp.concatenate(
        [block_of_rows, jnp.zeros((1, block_of_rows.shape[1]), jnp.bfloat16)], axis=0
    )
    selected_rows = padded[device_slots]
    reduced_rows = jnp.einsum(
        "hmb,hgb->hmg", selected_rows, adapter_down_weight, preferred_element_type=jnp.float32
    ).astype(jnp.bfloat16)
    every_slot = lax.all_gather(reduced_rows, "adapter", axis=0, tiled=True)
    slot_contributions = jnp.einsum(
        "qzf,qfo->qzo", every_slot, adapter_up_weight, preferred_element_type=jnp.float32
    )
    adapter_delta = slot_contributions.reshape(-1, adapter_up_weight.shape[2])[slot_per_request]
    device_query = (base_query + ADAPTER_SCALE * adapter_delta).astype(jnp.bfloat16)
    return (device_query, base_kv.astype(jnp.bfloat16))


def with_collectives(
    hidden,
    input_norm_gain,
    query_weight,
    key_value_weight,
    adapter_down_weight,
    adapter_up_weight,
    key_value_cache,
    valid_cache_lengths,
    request_per_slot,
    slot_per_request,
):
    owner_index = lax.axis_index("adapter")
    device_slots = lax.dynamic_slice_in_dim(request_per_slot, owner_index * ADP_DEV, ADP_DEV, 0)
    normed = rms_norm(hidden, input_norm_gain)
    query_steps = []
    keyvalue_steps = []
    for step_index in range(2):
        block_of_rows = lax.all_gather(normed[step_index], "adapter", axis=0, tiled=True)
        device_query, keyvalue_local = project_input(
            block_of_rows,
            query_weight,
            key_value_weight,
            adapter_down_weight,
            adapter_up_weight,
            device_slots,
            slot_per_request,
        )
        query_row_list, key_value_rows = (
            lax.all_to_all(device_query, "adapter", split_axis=0, concat_axis=1, tiled=True),
            lax.all_to_all(keyvalue_local, "adapter", split_axis=0, concat_axis=1, tiled=True),
        )
        query_steps.append(query_row_list)
        keyvalue_steps.append(key_value_rows)
    results = []
    fresh_keys_list = []
    latest_value_list = []
    for step_index in range(2):
        query_row_list = query_steps[step_index]
        key_value_rows = keyvalue_steps[step_index]
        token_positions = valid_cache_lengths + step_index
        rotated_query = apply_rotation(
            query_row_list.astype(jnp.float32), token_positions, QUERY_HEADS
        ).astype(jnp.bfloat16)
        incoming_key = apply_rotation(
            key_value_rows[:, : KEY_VALUE_HEADS * HEAD_SIZE].astype(jnp.float32),
            token_positions,
            KEY_VALUE_HEADS,
        ).astype(jnp.bfloat16)
        fresh_keys_list.append(incoming_key)
        latest_value_list.append(key_value_rows[:, KEY_VALUE_HEADS * HEAD_SIZE :])
        results.append(
            attend(
                rotated_query,
                key_value_cache,
                valid_cache_lengths,
                jnp.stack(fresh_keys_list, axis=1),
                jnp.stack(latest_value_list, axis=1),
            )
        )
    return jnp.stack(results)


MESH = pl.DeviceIdType.MESH
F32 = jnp.float32
BF16 = jnp.bfloat16


def block_kernel(
    parties,
    capacity,
    hidden_ref,
    gain_ref,
    query_weight_ref,
    key_value_weight_ref,
    down_ref,
    up_ref,
    cache_ref,
    length_ref,
    request_of_ref,
    slot_of_ref,
    out_ref,
    query_weight,
    key_value_weight,
    down,
    up,
    keys,
    values,
    gathered,
    spread_rows,
    rows,
    staged,
    ranks,
    pair_rows,
    pair_send,
    pair_received,
    result,
    local_sem,
    gather_send_sem,
    gather_sem,
    forward_send_sem,
    rank_send_sem,
    rank_sem,
    pair_send_sem,
    pair_sem,
):
    n = parties
    chips = n // 2
    width = rows.shape[1]
    blocks = width // HEAD_SIZE
    heads = query_weight.shape[1] // HEAD_SIZE
    total = keys.shape[0]
    me = lax.axis_index("adapter")
    core = lax.rem(me, 2)
    chip = me // 2
    sibling = chip * 2 + 1 - core

    loads = [
        (down_ref, down.at[pl.ds(0, ADAPTER_RANK)]),
        (down_ref, down.at[pl.ds(ADAPTER_RANK, ADAPTER_RANK)]),
        (query_weight_ref, query_weight),
        (key_value_weight_ref, key_value_weight),
        (up_ref, up),
        (cache_ref.at[0, 0], keys.at[pl.ds(0, capacity)]),
        (cache_ref.at[0, 1], values.at[pl.ds(0, capacity)]),
    ]
    copies = [
        pltpu.make_async_copy(source, target, local_sem.at[number])
        for number, (source, target) in enumerate(loads)
    ]

    barrier = pltpu.get_barrier_semaphore()

    def greet(k, carry):
        pl.semaphore_signal(
            barrier, inc=1, device_id={"adapter": lax.rem(me + k, n)}, device_id_type=MESH
        )
        return carry

    lax.fori_loop(1, n, greet, 0)
    for copy in copies:
        copy.start()

    for block in range(blocks):
        piece = hidden_ref[:, block * HEAD_SIZE : (block + 1) * HEAD_SIZE].astype(F32)
        for step in range(2):
            staged[pl.ds(step * blocks + block, 1), :] = piece[step : step + 1]
    for step in range(2):
        part = staged[step * blocks : (step + 1) * blocks, :]
        squares = jnp.sum(jnp.sum(part * part, axis=0, keepdims=True), axis=1, keepdims=True)
        part = part * lax.rsqrt(squares * (1.0 / width) + 1e-05) * gain_ref[...]
        gathered[me, step * blocks : (step + 1) * blocks, :] = part.astype(BF16)

    tail = total - capacity
    keys[capacity:, :] = jnp.zeros((tail, keys.shape[1]), BF16)
    values[capacity:, :] = jnp.zeros((tail, values.shape[1]), BF16)

    pl.semaphore_wait(barrier, n - 1)

    def own_copy(k):
        target = 2 * lax.rem(chip + k, chips) + core
        return pltpu.make_async_remote_copy(
            src_ref=gathered.at[me],
            dst_ref=gathered.at[me],
            send_sem=gather_send_sem.at[k],
            recv_sem=gather_sem.at[me],
            device_id={"adapter": target},
            device_id_type=MESH,
        )

    def sibling_copy(source):
        return pltpu.make_async_remote_copy(
            src_ref=gathered.at[source],
            dst_ref=gathered.at[source],
            send_sem=forward_send_sem.at[source // 2],
            recv_sem=gather_sem.at[source],
            device_id={"adapter": sibling},
            device_id_type=MESH,
        )

    def send_own(k, carry):
        own_copy(k).start()
        return carry

    lax.fori_loop(1, chips, send_own, 0)
    sibling_copy(me).start()

    def place(source):
        spread_rows[pl.ds(source, 2 * blocks, stride=n), :] = gathered[source].astype(F32)

    length = length_ref[0]
    row_index = lax.broadcasted_iota(jnp.int32, (24, HEAD_SIZE), 0)
    lane_index = lax.broadcasted_iota(jnp.int32, (24, HEAD_SIZE), 1)
    half = HEAD_SIZE // 2
    step_of_row = jnp.where(row_index < 16, (row_index // heads) % 2, row_index % 2)
    turn = (lane_index % half).astype(F32) * (-1.0 / half)
    frequency = jnp.exp(turn * math.log(ROPE_BASE))
    angles = (step_of_row + length).astype(F32) * frequency
    cosine = jnp.cos(angles)
    sine = jnp.sin(angles)
    sine = jnp.where(lane_index < half, -sine, sine)

    request_rows = lax.broadcasted_iota(jnp.int32, (n, HEAD_SIZE), 0)
    adapter_of = jnp.zeros((n, HEAD_SIZE), jnp.int32)
    for request in range(n):
        adapter_of = jnp.where(request_rows == request, slot_of_ref[request] // 2, adapter_of)
    mine = (request_rows == request_of_ref[me, 0]) | (request_rows == request_of_ref[me, 1])

    place(me)

    def forward(k, carry):
        source = 2 * lax.rem(chip + chips - k, chips) + core
        pltpu.make_async_remote_copy(
            src_ref=gathered.at[source],
            dst_ref=gathered.at[source],
            send_sem=gather_send_sem.at[0],
            recv_sem=gather_sem.at[source],
            device_id={"adapter": sibling},
            device_id_type=MESH,
        ).wait_recv()
        sibling_copy(source).start()
        place(source)
        return carry

    lax.fori_loop(1, chips, forward, 0)

    def take(k, carry):
        source = 2 * lax.rem(chip + chips - k, chips) + 1 - core
        sibling_copy(source).wait_recv()
        place(source)
        return carry

    lax.fori_loop(0, chips, take, 0)

    copies[0].wait()
    copies[1].wait()
    chunk = 1024
    per_chunk = chunk // HEAD_SIZE

    def shrink(c, acc):
        pieces = []
        for step in range(2):
            line = []
            for b in range(per_chunk):
                start = pl.multiple_of((step * blocks + c * per_chunk + b) * n, n)
                line.append(spread_rows[pl.ds(start, n), :].astype(BF16))
            pieces.append(jnp.concatenate(line, axis=1))
        piece = jnp.concatenate(pieces, axis=0)
        columns = pl.ds(pl.multiple_of(c * chunk, chunk), chunk)
        rows[:, columns] = piece
        return acc + lax.dot_general(
            piece, down[:, columns], (((1,), (1,)), ((), ())), preferred_element_type=F32
        )

    shrunk = lax.fori_loop(
        0, width // chunk, shrink, jnp.zeros((2 * n, 2 * ADAPTER_RANK), F32)
    )
    rank_lanes = lax.broadcasted_iota(jnp.int32, (n, HEAD_SIZE), 1)
    message = jnp.where(rank_lanes < ADAPTER_RANK, shrunk[:n], shrunk[n:])
    ranks[me] = jnp.where(mine, message, 0.0).astype(BF16)

    def rank_copy(k):
        return pltpu.make_async_remote_copy(
            src_ref=ranks.at[me],
            dst_ref=ranks.at[me],
            send_sem=rank_send_sem.at[k],
            recv_sem=rank_sem.at[me],
            device_id={"adapter": lax.rem(me + k, n)},
            device_id_type=MESH,
        )

    def send_rank(k, carry):
        rank_copy(k).start()
        return carry

    lax.fori_loop(1, n, send_rank, 0)

    copies[2].wait()
    copies[3].wait()

    def project(c, carry):
        query, keyvalue = carry
        columns = pl.ds(pl.multiple_of(c * chunk, chunk), chunk)
        piece = rows[:, columns]
        query = query + jnp.dot(piece, query_weight[columns, :], preferred_element_type=F32)
        keyvalue = keyvalue + jnp.dot(
            piece, key_value_weight[columns, :], preferred_element_type=F32
        )
        return query, keyvalue

    query, keyvalue = lax.fori_loop(
        0,
        width // chunk,
        project,
        (jnp.zeros((2 * n, query_weight.shape[1]), F32), jnp.zeros((2 * n, HEAD_SIZE), F32)),
    )
    for step in range(2):
        pair_rows[pl.ds(2 * heads + step, n, stride=16), :] = keyvalue[step * n : (step + 1) * n]

    copies[4].wait()

    def rank_arrival(k, carry):
        source = lax.rem(me + n - k, n)
        pltpu.make_async_remote_copy(
            src_ref=ranks.at[source],
            dst_ref=ranks.at[source],
            send_sem=rank_send_sem.at[0],
            recv_sem=rank_sem.at[source],
            device_id={"adapter": source},
            device_id_type=MESH,
        ).wait_recv()
        return carry

    lax.fori_loop(1, n, rank_arrival, 0)
    ranked = ranks[0].astype(F32)
    for source in range(1, n):
        ranked = ranked + ranks[source].astype(F32)
    turned = pltpu.roll(ranked, ADAPTER_RANK, 1)
    low = rank_lanes < ADAPTER_RANK
    both = jnp.concatenate(
        [jnp.where(low, ranked, turned), jnp.where(low, turned, ranked)], axis=0
    )
    adapter_rows = jnp.concatenate([adapter_of, adapter_of], axis=0)
    lane_half = lax.broadcasted_iota(jnp.int32, (2 * n, HEAD_SIZE), 1) // ADAPTER_RANK
    masked = [
        jnp.where(adapter_rows == 2 * pair + lane_half, both, 0.0).astype(BF16)
        for pair in range(n // 2)
    ]
    delta = jnp.dot(jnp.concatenate(masked, axis=1), up[...], preferred_element_type=F32)
    query = query + ADAPTER_SCALE * delta
    for step in range(2):
        for head in range(heads):
            pair_rows[pl.ds(step * heads + head, n, stride=16), :] = query[
                step * n : (step + 1) * n, head * HEAD_SIZE : (head + 1) * HEAD_SIZE
            ]
    for request in range(n):
        pair_send[request] = pair_rows[request * 16 : (request + 1) * 16, :].astype(BF16)

    def pair_copy(k):
        target = lax.rem(me + k, n)
        return pltpu.make_async_remote_copy(
            src_ref=pair_send.at[target],
            dst_ref=pair_received.at[me],
            send_sem=pair_send_sem.at[k],
            recv_sem=pair_sem.at[me],
            device_id={"adapter": target},
            device_id_type=MESH,
        )

    def send_pair(k, carry):
        pair_copy(k).start()
        return carry

    lax.fori_loop(1, n, send_pair, 0)
    pair_received[me] = pair_send[me]

    copies[5].wait()
    copies[6].wait()

    def pair_arrival(k, carry):
        source = lax.rem(me + n - k, n)
        pltpu.make_async_remote_copy(
            src_ref=pair_send.at[source],
            dst_ref=pair_received.at[source],
            send_sem=pair_send_sem.at[0],
            recv_sem=pair_sem.at[source],
            device_id={"adapter": source},
            device_id_type=MESH,
        ).wait_recv()
        return carry

    lax.fori_loop(1, n, pair_arrival, 0)

    columns = lax.broadcasted_iota(jnp.int32, (16, total), 1)
    steps = (lax.broadcasted_iota(jnp.int32, (16, total), 0) // heads) % 2
    valid = (columns < length) | ((columns >= capacity) & (columns - capacity <= steps))
    fresh = lax.broadcasted_iota(jnp.int32, (8, HEAD_SIZE), 0) < 2
    padding = jnp.zeros((8, HEAD_SIZE), F32)
    for group in range(KEY_VALUE_HEADS):
        lanes = slice(group * HEAD_SIZE, (group + 1) * HEAD_SIZE)
        key = pair_received[group].astype(F32)[8:]
        key = key * cosine[16:] + pltpu.roll(key, half, 1) * sine[16:]
        key = jnp.concatenate([jnp.where(fresh, key, 0.0), padding], axis=0)
        keys[capacity : capacity + 16, lanes] = key.astype(BF16)
        value = pair_received[KEY_VALUE_HEADS + group].astype(F32)[8:]
        value = jnp.concatenate([jnp.where(fresh, value, 0.0), padding], axis=0)
        values[capacity : capacity + 16, lanes] = value.astype(BF16)
        turned_query = jnp.concatenate(
            [
                pair_received[2 * group].astype(F32)[:8],
                pair_received[2 * group + 1].astype(F32)[:8],
            ],
            axis=0,
        )
        turned_query = turned_query * cosine[:16] + pltpu.roll(turned_query, half, 1) * sine[:16]
        scores = lax.dot_general(
            turned_query.astype(BF16),
            keys[:, lanes],
            (((1,), (1,)), ((), ())),
            preferred_element_type=F32,
        )
        scores = jnp.where(valid, scores * HEAD_SIZE ** (-0.5), -1e30)
        top = jnp.max(scores, axis=1, keepdims=True)
        weights = jnp.where(valid, jnp.exp(scores - top), 0.0)
        weights = weights / jnp.sum(weights, axis=1, keepdims=True)
        mixed = jnp.dot(weights.astype(BF16), values[:, lanes], preferred_element_type=F32)
        for side in range(2):
            for step in range(2):
                for head in range(heads):
                    start = ((2 * group + side) * heads + head) * HEAD_SIZE
                    line = (side * 2 + step) * heads + head
                    result[step : step + 1, start : start + HEAD_SIZE] = mixed[line : line + 1]
    out_ref[...] = result[...].astype(BF16)

    def finish(k, carry):
        rank_copy(k).wait_send()
        pair_copy(k).wait_send()
        return carry

    lax.fori_loop(1, n, finish, 0)

    def finish_gather(k, carry):
        own_copy(k).wait_send()
        return carry

    lax.fori_loop(1, chips, finish_gather, 0)

    def finish_forward(k, carry):
        sibling_copy(2 * k + core).wait_send()
        return carry

    lax.fori_loop(0, chips, finish_forward, 0)


def whole_block(
    hidden,
    input_norm_gain,
    query_weight,
    key_value_weight,
    adapter_down_weight,
    adapter_up_weight,
    key_value_cache,
    valid_cache_lengths,
    request_per_slot,
    slot_per_request,
):
    n = request_per_slot.shape[0]
    width = hidden.shape[2]
    blocks = width // HEAD_SIZE
    capacity = key_value_cache.shape[2]
    kv_width = key_value_cache.shape[3]
    total = capacity + HEAD_SIZE
    columns = query_weight.shape[1]
    anywhere = pl.BlockSpec(memory_space=pl.ANY)
    in_vmem = pl.BlockSpec(memory_space=pltpu.VMEM)
    in_smem = pl.BlockSpec(memory_space=pltpu.SMEM)
    dma = pltpu.SemaphoreType.DMA
    call = pl.pallas_call(
        functools.partial(block_kernel, n, capacity),
        out_shape=jax.ShapeDtypeStruct((2, width), BF16),
        in_specs=[in_vmem, in_vmem] + [anywhere] * 5 + [in_smem] * 3,
        out_specs=in_vmem,
        scratch_shapes=[
            pltpu.VMEM((width, columns), BF16),
            pltpu.VMEM((width, HEAD_SIZE), BF16),
            pltpu.VMEM((2 * ADAPTER_RANK, width), BF16),
            pltpu.VMEM((n * ADAPTER_RANK, columns), BF16),
            pltpu.VMEM((total, kv_width), BF16),
            pltpu.VMEM((total, kv_width), BF16),
            pltpu.VMEM((n, 2 * blocks, HEAD_SIZE), BF16),
            pltpu.VMEM((2 * blocks * n, HEAD_SIZE), F32),
            pltpu.VMEM((2 * n, width), BF16),
            pltpu.VMEM((2 * blocks, HEAD_SIZE), F32),
            pltpu.VMEM((n, n, HEAD_SIZE), BF16),
            pltpu.VMEM((n * 16, HEAD_SIZE), F32),
            pltpu.VMEM((n, 16, HEAD_SIZE), BF16),
            pltpu.VMEM((n, 16, HEAD_SIZE), BF16),
            pltpu.VMEM((2, width), F32),
            dma((7,)),
            dma((n // 2,)),
            dma((n,)),
            dma((n // 2,)),
            dma((n,)),
            dma((n,)),
            dma((n,)),
            dma((n,)),
        ],
        compiler_params=pltpu.CompilerParams(
            collective_id=0, has_side_effects=True, vmem_limit_bytes=40 * 2 ** 20
        ),
        name="decode_block",
    )
    out = call(
        hidden.reshape(2, width),
        input_norm_gain.reshape(blocks, HEAD_SIZE),
        query_weight,
        key_value_weight,
        adapter_down_weight.reshape(ADAPTER_RANK, width),
        adapter_up_weight.reshape(n * ADAPTER_RANK, columns),
        key_value_cache,
        valid_cache_lengths,
        request_per_slot,
        slot_per_request,
    )
    return out.reshape(2, 1, width)


def on_device(*arguments):
    hidden, _, query_weight, key_value_weight, _, _, _, _, request_per_slot, _ = arguments
    fits = (
        hidden.shape[1] == 1
        and key_value_weight.shape[1] == HEAD_SIZE
        and query_weight.shape[1] == 4 * HEAD_SIZE
        and request_per_slot.shape[0] == 16
    )
    return whole_block(*arguments) if fits else with_collectives(*arguments)


def solution(mesh):
    in_specs = (
        P(None, ("replica", "adapter"), None),
        P(),
        P(None, "adapter"),
        P(None, "adapter"),
        P(("replica", "adapter"), None, None),
        P("replica", None, "adapter"),
        P(("replica", "adapter"), None, None, None),
        P(("replica", "adapter")),
        P("replica", None),
        P("replica"),
    )
    out_specs = P(None, ("replica", "adapter"), None)
    return jax.shard_map(
        on_device, mesh=mesh, in_specs=in_specs, out_specs=out_specs, check_vma=False
    )
```

```python
import functools
import math

import jax
import jax.numpy as jnp
from jax import lax
from jax.experimental import pallas as pl
from jax.experimental.pallas import tpu as pltpu
from jax.sharding import PartitionSpec as P

QUERY_HEADS = 64
KEY_VALUE_HEADS = 8
HEAD_SIZE = 128
ADP_DEV = 1
ADAPTER_RANK = 64


ADAPTER_SCALE = 0.5
ROPE_BASE = 500000.0


def rms_norm(hidden_rows, input_norm_gain):
    values = hidden_rows.astype(jnp.float32)
    spread = jnp.mean(values * values, axis=-1, keepdims=True)
    return (values * lax.rsqrt(spread + 1e-05) * input_norm_gain).astype(jnp.bfloat16)


def apply_rotation(values, token_positions, heads):
    batch_row_list = values.shape[0]
    shaped = values.reshape(batch_row_list, heads, -1)
    half_dim = shaped.shape[-1] // 2
    frequency = ROPE_BASE ** (-jnp.arange(half_dim, dtype=jnp.float32) / half_dim)
    angles = token_positions.astype(jnp.float32)[:, None, None] * frequency[None, None, :]
    cosine = jnp.cos(angles)
    sine_part = jnp.sin(angles)
    first = shaped[..., :half_dim]
    second = shaped[..., half_dim:]
    turned = jnp.concatenate(
        [first * cosine - second * sine_part, second * cosine + first * sine_part], axis=-1
    )
    return turned.reshape(batch_row_list, -1)


def attend(query_row_list, block_of_cache, lengths, latest_keys, latest_values):
    batch_row_list = query_row_list.shape[0]
    query_matrix = query_row_list.reshape(
        batch_row_list, KEY_VALUE_HEADS, QUERY_HEADS // KEY_VALUE_HEADS, HEAD_SIZE
    )
    cached_key_rows = block_of_cache[:, 0].reshape(batch_row_list, -1, KEY_VALUE_HEADS, HEAD_SIZE)
    cached_value_rows = block_of_cache[:, 1].reshape(batch_row_list, -1, KEY_VALUE_HEADS, HEAD_SIZE)
    appended_keys = latest_keys.reshape(batch_row_list, -1, KEY_VALUE_HEADS, HEAD_SIZE)
    appended_values = latest_values.reshape(batch_row_list, -1, KEY_VALUE_HEADS, HEAD_SIZE)
    score_scale = HEAD_SIZE ** (-0.5)
    old_scores = (
        jnp.einsum(
            "bhgd,blhd->bhgl", query_matrix, cached_key_rows, preferred_element_type=jnp.float32
        )
        * score_scale
    )
    valid_mask = (jnp.arange(cached_key_rows.shape[1])[None, :] < lengths[:, None])[
        :, None, None, :
    ]
    old_scores = jnp.where(valid_mask, old_scores, -1e30)
    new_scores = (
        jnp.einsum(
            "bhgd,bshd->bhgs", query_matrix, appended_keys, preferred_element_type=jnp.float32
        )
        * score_scale
    )
    row_top = jnp.maximum(jnp.max(old_scores, axis=-1), jnp.max(new_scores, axis=-1))[..., None]
    old_weights = jnp.where(valid_mask, jnp.exp(old_scores - row_top), 0.0)
    new_weights = jnp.exp(new_scores - row_top)
    weight_total = jnp.sum(old_weights, axis=-1, keepdims=True) + jnp.sum(
        new_weights, axis=-1, keepdims=True
    )
    old_probs = (old_weights / weight_total).astype(jnp.bfloat16)
    new_probs = (new_weights / weight_total).astype(jnp.bfloat16)
    mixed = jnp.einsum(
        "bhgl,blhd->bhgd", old_probs, cached_value_rows, preferred_element_type=jnp.float32
    )
    mixed = mixed + jnp.einsum(
        "bhgs,bshd->bhgd", new_probs, appended_values, preferred_element_type=jnp.float32
    )
    return mixed.reshape(batch_row_list, -1).astype(jnp.bfloat16)


def project_input(
    block_of_rows,
    query_weight,
    key_value_weight,
    adapter_down_weight,
    adapter_up_weight,
    device_slots,
    slot_per_request,
):
    base_query = jnp.dot(block_of_rows, query_weight, preferred_element_type=jnp.float32)
    base_kv = jnp.dot(block_of_rows, key_value_weight, preferred_element_type=jnp.float32)
    padded = jnp.concatenate(
        [block_of_rows, jnp.zeros((1, block_of_rows.shape[1]), jnp.bfloat16)], axis=0
    )
    selected_rows = padded[device_slots]
    reduced_rows = jnp.einsum(
        "hmb,hgb->hmg", selected_rows, adapter_down_weight, preferred_element_type=jnp.float32
    ).astype(jnp.bfloat16)
    every_slot = lax.all_gather(reduced_rows, "adapter", axis=0, tiled=True)
    slot_contributions = jnp.einsum(
        "qzf,qfo->qzo", every_slot, adapter_up_weight, preferred_element_type=jnp.float32
    )
    adapter_delta = slot_contributions.reshape(-1, adapter_up_weight.shape[2])[slot_per_request]
    device_query = (base_query + ADAPTER_SCALE * adapter_delta).astype(jnp.bfloat16)
    return (device_query, base_kv.astype(jnp.bfloat16))


def with_collectives(
    hidden,
    input_norm_gain,
    query_weight,
    key_value_weight,
    adapter_down_weight,
    adapter_up_weight,
    key_value_cache,
    valid_cache_lengths,
    request_per_slot,
    slot_per_request,
):
    owner_index = lax.axis_index("adapter")
    device_slots = lax.dynamic_slice_in_dim(request_per_slot, owner_index * ADP_DEV, ADP_DEV, 0)
    normed = rms_norm(hidden, input_norm_gain)
    query_steps = []
    keyvalue_steps = []
    for step_index in range(2):
        block_of_rows = lax.all_gather(normed[step_index], "adapter", axis=0, tiled=True)
        device_query, keyvalue_local = project_input(
            block_of_rows,
            query_weight,
            key_value_weight,
            adapter_down_weight,
            adapter_up_weight,
            device_slots,
            slot_per_request,
        )
        query_row_list, key_value_rows = (
            lax.all_to_all(device_query, "adapter", split_axis=0, concat_axis=1, tiled=True),
            lax.all_to_all(keyvalue_local, "adapter", split_axis=0, concat_axis=1, tiled=True),
        )
        query_steps.append(query_row_list)
        keyvalue_steps.append(key_value_rows)
    results = []
    fresh_keys_list = []
    latest_value_list = []
    for step_index in range(2):
        query_row_list = query_steps[step_index]
        key_value_rows = keyvalue_steps[step_index]
        token_positions = valid_cache_lengths + step_index
        rotated_query = apply_rotation(
            query_row_list.astype(jnp.float32), token_positions, QUERY_HEADS
        ).astype(jnp.bfloat16)
        incoming_key = apply_rotation(
            key_value_rows[:, : KEY_VALUE_HEADS * HEAD_SIZE].astype(jnp.float32),
            token_positions,
            KEY_VALUE_HEADS,
        ).astype(jnp.bfloat16)
        fresh_keys_list.append(incoming_key)
        latest_value_list.append(key_value_rows[:, KEY_VALUE_HEADS * HEAD_SIZE :])
        results.append(
            attend(
                rotated_query,
                key_value_cache,
                valid_cache_lengths,
                jnp.stack(fresh_keys_list, axis=1),
                jnp.stack(latest_value_list, axis=1),
            )
        )
    return jnp.stack(results)


MESH = pl.DeviceIdType.MESH
F32 = jnp.float32
BF16 = jnp.bfloat16


def block_kernel(
    parties,
    capacity,
    hidden_ref,
    gain_ref,
    query_weight_ref,
    key_value_weight_ref,
    down_ref,
    up_ref,
    cache_ref,
    length_source,
    request_of_source,
    slot_of_source,
    out_ref,
    length_ref,
    request_of_ref,
    slot_of_ref,
    hidden,
    gain,
    query_weight,
    key_value_weight,
    down,
    up,
    keys,
    values,
    gathered,
    spread_rows,
    rows,
    staged,
    ranks,
    pair_rows,
    pair_send,
    pair_received,
    result,
    local_sem,
    gather_send_sem,
    gather_sem,
    forward_send_sem,
    rank_send_sem,
    rank_sem,
    pair_send_sem,
    pair_sem,
):
    n = parties
    chips = n // 2
    width = rows.shape[1]
    blocks = width // HEAD_SIZE
    heads = query_weight.shape[1] // HEAD_SIZE
    total = keys.shape[0]
    me = lax.axis_index("adapter")
    core = lax.rem(me, 2)
    chip = me // 2
    sibling = chip * 2 + 1 - core

    loads = [
        (down_ref, down.at[pl.ds(0, ADAPTER_RANK)]),
        (down_ref, down.at[pl.ds(ADAPTER_RANK, ADAPTER_RANK)]),
        (query_weight_ref, query_weight),
        (key_value_weight_ref, key_value_weight),
        (up_ref, up),
        (cache_ref.at[0, 0], keys.at[pl.ds(0, capacity)]),
        (cache_ref.at[0, 1], values.at[pl.ds(0, capacity)]),
        (hidden_ref, hidden),
        (gain_ref, gain),
        (length_source, length_ref),
        (request_of_source, request_of_ref),
        (slot_of_source, slot_of_ref),
    ]
    copies = [
        pltpu.make_async_copy(source, target, local_sem.at[number])
        for number, (source, target) in enumerate(loads)
    ]

    for copy in copies[7:]:
        copy.start()
    barrier = pltpu.get_barrier_semaphore()

    def greet(k, carry):
        pl.semaphore_signal(
            barrier, inc=1, device_id={"adapter": lax.rem(me + k, n)}, device_id_type=MESH
        )
        return carry

    lax.fori_loop(1, n, greet, 0)
    for copy in copies[:7]:
        copy.start()
    copies[7].wait()
    copies[8].wait()

    for block in range(blocks):
        piece = hidden[:, block * HEAD_SIZE : (block + 1) * HEAD_SIZE].astype(F32)
        for step in range(2):
            staged[pl.ds(step * blocks + block, 1), :] = piece[step : step + 1]
    for step in range(2):
        part = staged[step * blocks : (step + 1) * blocks, :]
        squares = jnp.sum(jnp.sum(part * part, axis=0, keepdims=True), axis=1, keepdims=True)
        part = part * lax.rsqrt(squares * (1.0 / width) + 1e-05) * gain[...]
        gathered[me, step * blocks : (step + 1) * blocks, :] = part.astype(BF16)

    tail = total - capacity
    keys[capacity:, :] = jnp.zeros((tail, keys.shape[1]), BF16)
    values[capacity:, :] = jnp.zeros((tail, values.shape[1]), BF16)

    pl.semaphore_wait(barrier, n - 1)

    def own_copy(k):
        target = 2 * lax.rem(chip + k, chips) + core
        return pltpu.make_async_remote_copy(
            src_ref=gathered.at[me],
            dst_ref=gathered.at[me],
            send_sem=gather_send_sem.at[k],
            recv_sem=gather_sem.at[me],
            device_id={"adapter": target},
            device_id_type=MESH,
        )

    def sibling_copy(source):
        return pltpu.make_async_remote_copy(
            src_ref=gathered.at[source],
            dst_ref=gathered.at[source],
            send_sem=forward_send_sem.at[source // 2],
            recv_sem=gather_sem.at[source],
            device_id={"adapter": sibling},
            device_id_type=MESH,
        )

    def send_own(k, carry):
        own_copy(k).start()
        return carry

    lax.fori_loop(1, chips, send_own, 0)
    sibling_copy(me).start()

    def place(source):
        spread_rows[pl.ds(source, 2 * blocks, stride=n), :] = gathered[source].astype(F32)

    for copy in copies[9:]:
        copy.wait()
    length = length_ref[0]
    row_index = lax.broadcasted_iota(jnp.int32, (24, HEAD_SIZE), 0)
    lane_index = lax.broadcasted_iota(jnp.int32, (24, HEAD_SIZE), 1)
    half = HEAD_SIZE // 2
    step_of_row = jnp.where(row_index < 16, (row_index // heads) % 2, row_index % 2)
    turn = (lane_index % half).astype(F32) * (-1.0 / half)
    frequency = jnp.exp(turn * math.log(ROPE_BASE))
    angles = (step_of_row + length).astype(F32) * frequency
    cosine = jnp.cos(angles)
    sine = jnp.sin(angles)
    sine = jnp.where(lane_index < half, -sine, sine)

    request_rows = lax.broadcasted_iota(jnp.int32, (n, HEAD_SIZE), 0)
    adapter_of = jnp.zeros((n, HEAD_SIZE), jnp.int32)
    for request in range(n):
        adapter_of = jnp.where(request_rows == request, slot_of_ref[request] // 2, adapter_of)
    mine = (request_rows == request_of_ref[0, me]) | (request_rows == request_of_ref[1, me])

    place(me)

    def forward(k, carry):
        source = 2 * lax.rem(chip + chips - k, chips) + core
        pltpu.make_async_remote_copy(
            src_ref=gathered.at[source],
            dst_ref=gathered.at[source],
            send_sem=gather_send_sem.at[0],
            recv_sem=gather_sem.at[source],
            device_id={"adapter": sibling},
            device_id_type=MESH,
        ).wait_recv()
        sibling_copy(source).start()
        place(source)
        return carry

    lax.fori_loop(1, chips, forward, 0)

    def take(k, carry):
        source = 2 * lax.rem(chip + chips - k, chips) + 1 - core
        sibling_copy(source).wait_recv()
        place(source)
        return carry

    lax.fori_loop(0, chips, take, 0)

    copies[0].wait()
    copies[1].wait()
    chunk = 4096
    per_chunk = chunk // HEAD_SIZE

    def shrink(c, acc):
        pieces = []
        for step in range(2):
            line = []
            for b in range(per_chunk):
                start = pl.multiple_of((step * blocks + c * per_chunk + b) * n, n)
                line.append(spread_rows[pl.ds(start, n), :].astype(BF16))
            pieces.append(jnp.concatenate(line, axis=1))
        piece = jnp.concatenate(pieces, axis=0)
        columns = pl.ds(pl.multiple_of(c * chunk, chunk), chunk)
        rows[:, columns] = piece
        return acc + lax.dot_general(
            piece, down[:, columns], (((1,), (1,)), ((), ())), preferred_element_type=F32
        )

    shrunk = lax.fori_loop(
        0, width // chunk, shrink, jnp.zeros((2 * n, 2 * ADAPTER_RANK), F32)
    )
    rank_lanes = lax.broadcasted_iota(jnp.int32, (n, HEAD_SIZE), 1)
    message = jnp.where(rank_lanes < ADAPTER_RANK, shrunk[:n], shrunk[n:])
    ranks[me] = jnp.where(mine, message, 0.0).astype(BF16)

    def rank_copy(k):
        return pltpu.make_async_remote_copy(
            src_ref=ranks.at[me],
            dst_ref=ranks.at[me],
            send_sem=rank_send_sem.at[k],
            recv_sem=rank_sem.at[me],
            device_id={"adapter": lax.rem(me + k, n)},
            device_id_type=MESH,
        )

    def send_rank(k, carry):
        rank_copy(k).start()
        return carry

    lax.fori_loop(1, n, send_rank, 0)

    copies[2].wait()
    copies[3].wait()

    def project(c, carry):
        query, keyvalue = carry
        columns = pl.ds(pl.multiple_of(c * chunk, chunk), chunk)
        piece = rows[:, columns]
        query = query + jnp.dot(piece, query_weight[columns, :], preferred_element_type=F32)
        keyvalue = keyvalue + jnp.dot(
            piece, key_value_weight[columns, :], preferred_element_type=F32
        )
        return query, keyvalue

    query, keyvalue = lax.fori_loop(
        0,
        width // chunk,
        project,
        (jnp.zeros((2 * n, query_weight.shape[1]), F32), jnp.zeros((2 * n, HEAD_SIZE), F32)),
    )
    for step in range(2):
        pair_rows[pl.ds(2 * heads + step, n, stride=16), :] = keyvalue[step * n : (step + 1) * n]

    copies[4].wait()

    def rank_arrival(k, carry):
        source = lax.rem(me + n - k, n)
        pltpu.make_async_remote_copy(
            src_ref=ranks.at[source],
            dst_ref=ranks.at[source],
            send_sem=rank_send_sem.at[0],
            recv_sem=rank_sem.at[source],
            device_id={"adapter": source},
            device_id_type=MESH,
        ).wait_recv()
        return carry

    lax.fori_loop(1, n, rank_arrival, 0)
    ranked = ranks[0].astype(F32)
    for source in range(1, n):
        ranked = ranked + ranks[source].astype(F32)
    turned = pltpu.roll(ranked, ADAPTER_RANK, 1)
    low = rank_lanes < ADAPTER_RANK
    both = jnp.concatenate(
        [jnp.where(low, ranked, turned), jnp.where(low, turned, ranked)], axis=0
    )
    adapter_rows = jnp.concatenate([adapter_of, adapter_of], axis=0)
    lane_half = lax.broadcasted_iota(jnp.int32, (2 * n, HEAD_SIZE), 1) // ADAPTER_RANK
    masked = [
        jnp.where(adapter_rows == 2 * pair + lane_half, both, 0.0).astype(BF16)
        for pair in range(n // 2)
    ]
    delta = jnp.dot(jnp.concatenate(masked, axis=1), up[...], preferred_element_type=F32)
    query = query + ADAPTER_SCALE * delta
    for step in range(2):
        for head in range(heads):
            pair_rows[pl.ds(step * heads + head, n, stride=16), :] = query[
                step * n : (step + 1) * n, head * HEAD_SIZE : (head + 1) * HEAD_SIZE
            ]
    for request in range(n):
        pair_send[request] = pair_rows[request * 16 : (request + 1) * 16, :].astype(BF16)

    def pair_copy(k):
        target = lax.rem(me + k, n)
        return pltpu.make_async_remote_copy(
            src_ref=pair_send.at[target],
            dst_ref=pair_received.at[me],
            send_sem=pair_send_sem.at[k],
            recv_sem=pair_sem.at[me],
            device_id={"adapter": target},
            device_id_type=MESH,
        )

    def send_pair(k, carry):
        pair_copy(k).start()
        return carry

    lax.fori_loop(1, n, send_pair, 0)
    pair_received[me] = pair_send[me]

    copies[5].wait()
    copies[6].wait()

    def finish_ranks(k, carry):
        rank_copy(k).wait_send()
        return carry

    lax.fori_loop(1, n, finish_ranks, 0)

    def finish_gather(k, carry):
        own_copy(k).wait_send()
        return carry

    lax.fori_loop(1, chips, finish_gather, 0)

    def finish_forward(k, carry):
        sibling_copy(2 * k + core).wait_send()
        return carry

    lax.fori_loop(0, chips, finish_forward, 0)

    def pair_arrival(k, carry):
        source = lax.rem(me + n - k, n)
        pltpu.make_async_remote_copy(
            src_ref=pair_send.at[source],
            dst_ref=pair_received.at[source],
            send_sem=pair_send_sem.at[0],
            recv_sem=pair_sem.at[source],
            device_id={"adapter": source},
            device_id_type=MESH,
        ).wait_recv()
        return carry

    lax.fori_loop(1, n, pair_arrival, 0)

    columns = lax.broadcasted_iota(jnp.int32, (16, total), 1)
    steps = (lax.broadcasted_iota(jnp.int32, (16, total), 0) // heads) % 2
    valid = (columns < length) | ((columns >= capacity) & (columns - capacity <= steps))
    fresh = lax.broadcasted_iota(jnp.int32, (8, HEAD_SIZE), 0) < 2
    padding = jnp.zeros((8, HEAD_SIZE), F32)
    turned_queries = []
    for group in range(KEY_VALUE_HEADS):
        turned_query = jnp.concatenate(
            [
                pair_received[2 * group].astype(F32)[:8],
                pair_received[2 * group + 1].astype(F32)[:8],
            ],
            axis=0,
        )
        turned_query = turned_query * cosine[:16] + pltpu.roll(turned_query, half, 1) * sine[:16]
        turned_queries.append(turned_query.astype(BF16))
    new_keys = []
    new_values = []
    for group in range(KEY_VALUE_HEADS):
        key = pair_received[group].astype(F32)[8:]
        key = key * cosine[16:] + pltpu.roll(key, half, 1) * sine[16:]
        key = jnp.concatenate([jnp.where(fresh, key, 0.0), padding], axis=0)
        new_keys.append(key.astype(BF16))
        value = pair_received[KEY_VALUE_HEADS + group].astype(F32)[8:]
        value = jnp.concatenate([jnp.where(fresh, value, 0.0), padding], axis=0)
        new_values.append(value.astype(BF16))
    keys[capacity : capacity + 16, :] = jnp.concatenate(new_keys, axis=1)
    values[capacity : capacity + 16, :] = jnp.concatenate(new_values, axis=1)
    scores = [
        lax.dot_general(
            turned_queries[group],
            keys[:, group * HEAD_SIZE : (group + 1) * HEAD_SIZE],
            (((1,), (1,)), ((), ())),
            preferred_element_type=F32,
        )
        for group in range(KEY_VALUE_HEADS)
    ]
    scores = [jnp.where(valid, part * HEAD_SIZE ** (-0.5), -1e30) for part in scores]
    tops = [jnp.max(part, axis=1, keepdims=True) for part in scores]
    weights = [
        jnp.where(valid, jnp.exp(part - top), 0.0) for part, top in zip(scores, tops)
    ]
    sums = [jnp.sum(part, axis=1, keepdims=True) for part in weights]
    weights = [(part / whole).astype(BF16) for part, whole in zip(weights, sums)]
    mixed = [
        jnp.dot(
            weights[group],
            values[:, group * HEAD_SIZE : (group + 1) * HEAD_SIZE],
            preferred_element_type=F32,
        )
        for group in range(KEY_VALUE_HEADS)
    ]
    for group in range(KEY_VALUE_HEADS):
        for side in range(2):
            for step in range(2):
                for head in range(heads):
                    start = ((2 * group + side) * heads + head) * HEAD_SIZE
                    line = (side * 2 + step) * heads + head
                    result[step : step + 1, start : start + HEAD_SIZE] = mixed[group][
                        line : line + 1
                    ]
    out_ref[...] = result[...].astype(BF16)

    def finish(k, carry):
        pair_copy(k).wait_send()
        return carry

    lax.fori_loop(1, n, finish, 0)


def whole_block(
    hidden,
    input_norm_gain,
    query_weight,
    key_value_weight,
    adapter_down_weight,
    adapter_up_weight,
    key_value_cache,
    valid_cache_lengths,
    request_per_slot,
    slot_per_request,
):
    n = request_per_slot.shape[0]
    width = hidden.shape[2]
    blocks = width // HEAD_SIZE
    capacity = key_value_cache.shape[2]
    kv_width = key_value_cache.shape[3]
    total = capacity + HEAD_SIZE
    columns = query_weight.shape[1]
    in_hbm = pl.BlockSpec(memory_space=pltpu.HBM)
    in_vmem = pl.BlockSpec(memory_space=pltpu.VMEM)
    dma = pltpu.SemaphoreType.DMA
    call = pl.pallas_call(
        functools.partial(block_kernel, n, capacity),
        out_shape=jax.ShapeDtypeStruct((2, width), BF16),
        in_specs=[in_hbm] * 10,
        out_specs=in_vmem,
        scratch_shapes=[
            pltpu.SMEM(valid_cache_lengths.shape, jnp.int32),
            pltpu.SMEM(request_per_slot.shape[::-1], jnp.int32),
            pltpu.SMEM(slot_per_request.shape, jnp.int32),
            pltpu.VMEM((2, width), BF16),
            pltpu.VMEM((blocks, HEAD_SIZE), F32),
            pltpu.VMEM((width, columns), BF16),
            pltpu.VMEM((width, HEAD_SIZE), BF16),
            pltpu.VMEM((2 * ADAPTER_RANK, width), BF16),
            pltpu.VMEM((n * ADAPTER_RANK, columns), BF16),
            pltpu.VMEM((total, kv_width), BF16),
            pltpu.VMEM((total, kv_width), BF16),
            pltpu.VMEM((n, 2 * blocks, HEAD_SIZE), BF16),
            pltpu.VMEM((2 * blocks * n, HEAD_SIZE), F32),
            pltpu.VMEM((2 * n, width), BF16),
            pltpu.VMEM((2 * blocks, HEAD_SIZE), F32),
            pltpu.VMEM((n, n, HEAD_SIZE), BF16),
            pltpu.VMEM((n * 16, HEAD_SIZE), F32),
            pltpu.VMEM((n, 16, HEAD_SIZE), BF16),
            pltpu.VMEM((n, 16, HEAD_SIZE), BF16),
            pltpu.VMEM((2, width), F32),
            dma((12,)),
            dma((n // 2,)),
            dma((n,)),
            dma((n // 2,)),
            dma((n,)),
            dma((n,)),
            dma((n,)),
            dma((n,)),
        ],
        compiler_params=pltpu.CompilerParams(
            collective_id=0, has_side_effects=True, vmem_limit_bytes=63 * 2 ** 20
        ),
        name="decode_block",
    )
    out = call(
        hidden.reshape(2, width),
        input_norm_gain.reshape(blocks, HEAD_SIZE),
        query_weight,
        key_value_weight,
        adapter_down_weight.reshape(ADAPTER_RANK, width),
        adapter_up_weight.reshape(n * ADAPTER_RANK, columns),
        key_value_cache,
        valid_cache_lengths,
        request_per_slot.T,
        slot_per_request,
    )
    return out.reshape(2, 1, width)


def on_device(*arguments):
    hidden, _, query_weight, key_value_weight, _, _, _, _, request_per_slot, _ = arguments
    fits = (
        hidden.shape[1] == 1
        and key_value_weight.shape[1] == HEAD_SIZE
        and query_weight.shape[1] == 4 * HEAD_SIZE
        and request_per_slot.shape[0] == 16
    )
    return whole_block(*arguments) if fits else with_collectives(*arguments)


def solution(mesh):
    in_specs = (
        P(None, ("replica", "adapter"), None),
        P(),
        P(None, "adapter"),
        P(None, "adapter"),
        P(("replica", "adapter"), None, None),
        P("replica", None, "adapter"),
        P(("replica", "adapter"), None, None, None),
        P(("replica", "adapter")),
        P("replica", None),
        P("replica"),
    )
    out_specs = P(None, ("replica", "adapter"), None)
    return jax.shard_map(
        on_device, mesh=mesh, in_specs=in_specs, out_specs=out_specs, check_vma=False
    )
```

```python
import functools
import math

import jax
import jax.numpy as jnp
from jax import lax
from jax.experimental import pallas as pl
from jax.experimental.pallas import tpu as pltpu
from jax.sharding import PartitionSpec as P

QUERY_HEADS = 64
KEY_VALUE_HEADS = 8
HEAD_SIZE = 128
ADP_DEV = 1
ADAPTER_RANK = 64


ADAPTER_SCALE = 0.5
ROPE_BASE = 500000.0


def rms_norm(hidden_rows, input_norm_gain):
    values = hidden_rows.astype(jnp.float32)
    spread = jnp.mean(values * values, axis=-1, keepdims=True)
    return (values * lax.rsqrt(spread + 1e-05) * input_norm_gain).astype(jnp.bfloat16)


def apply_rotation(values, token_positions, heads):
    batch_row_list = values.shape[0]
    shaped = values.reshape(batch_row_list, heads, -1)
    half_dim = shaped.shape[-1] // 2
    frequency = ROPE_BASE ** (-jnp.arange(half_dim, dtype=jnp.float32) / half_dim)
    angles = token_positions.astype(jnp.float32)[:, None, None] * frequency[None, None, :]
    cosine = jnp.cos(angles)
    sine_part = jnp.sin(angles)
    first = shaped[..., :half_dim]
    second = shaped[..., half_dim:]
    turned = jnp.concatenate(
        [first * cosine - second * sine_part, second * cosine + first * sine_part], axis=-1
    )
    return turned.reshape(batch_row_list, -1)


def attend(query_row_list, block_of_cache, lengths, latest_keys, latest_values):
    batch_row_list = query_row_list.shape[0]
    query_matrix = query_row_list.reshape(
        batch_row_list, KEY_VALUE_HEADS, QUERY_HEADS // KEY_VALUE_HEADS, HEAD_SIZE
    )
    cached_key_rows = block_of_cache[:, 0].reshape(batch_row_list, -1, KEY_VALUE_HEADS, HEAD_SIZE)
    cached_value_rows = block_of_cache[:, 1].reshape(batch_row_list, -1, KEY_VALUE_HEADS, HEAD_SIZE)
    appended_keys = latest_keys.reshape(batch_row_list, -1, KEY_VALUE_HEADS, HEAD_SIZE)
    appended_values = latest_values.reshape(batch_row_list, -1, KEY_VALUE_HEADS, HEAD_SIZE)
    score_scale = HEAD_SIZE ** (-0.5)
    old_scores = (
        jnp.einsum(
            "bhgd,blhd->bhgl", query_matrix, cached_key_rows, preferred_element_type=jnp.float32
        )
        * score_scale
    )
    valid_mask = (jnp.arange(cached_key_rows.shape[1])[None, :] < lengths[:, None])[
        :, None, None, :
    ]
    old_scores = jnp.where(valid_mask, old_scores, -1e30)
    new_scores = (
        jnp.einsum(
            "bhgd,bshd->bhgs", query_matrix, appended_keys, preferred_element_type=jnp.float32
        )
        * score_scale
    )
    row_top = jnp.maximum(jnp.max(old_scores, axis=-1), jnp.max(new_scores, axis=-1))[..., None]
    old_weights = jnp.where(valid_mask, jnp.exp(old_scores - row_top), 0.0)
    new_weights = jnp.exp(new_scores - row_top)
    weight_total = jnp.sum(old_weights, axis=-1, keepdims=True) + jnp.sum(
        new_weights, axis=-1, keepdims=True
    )
    old_probs = (old_weights / weight_total).astype(jnp.bfloat16)
    new_probs = (new_weights / weight_total).astype(jnp.bfloat16)
    mixed = jnp.einsum(
        "bhgl,blhd->bhgd", old_probs, cached_value_rows, preferred_element_type=jnp.float32
    )
    mixed = mixed + jnp.einsum(
        "bhgs,bshd->bhgd", new_probs, appended_values, preferred_element_type=jnp.float32
    )
    return mixed.reshape(batch_row_list, -1).astype(jnp.bfloat16)


def project_input(
    block_of_rows,
    query_weight,
    key_value_weight,
    adapter_down_weight,
    adapter_up_weight,
    device_slots,
    slot_per_request,
):
    base_query = jnp.dot(block_of_rows, query_weight, preferred_element_type=jnp.float32)
    base_kv = jnp.dot(block_of_rows, key_value_weight, preferred_element_type=jnp.float32)
    padded = jnp.concatenate(
        [block_of_rows, jnp.zeros((1, block_of_rows.shape[1]), jnp.bfloat16)], axis=0
    )
    selected_rows = padded[device_slots]
    reduced_rows = jnp.einsum(
        "hmb,hgb->hmg", selected_rows, adapter_down_weight, preferred_element_type=jnp.float32
    ).astype(jnp.bfloat16)
    every_slot = lax.all_gather(reduced_rows, "adapter", axis=0, tiled=True)
    slot_contributions = jnp.einsum(
        "qzf,qfo->qzo", every_slot, adapter_up_weight, preferred_element_type=jnp.float32
    )
    adapter_delta = slot_contributions.reshape(-1, adapter_up_weight.shape[2])[slot_per_request]
    device_query = (base_query + ADAPTER_SCALE * adapter_delta).astype(jnp.bfloat16)
    return (device_query, base_kv.astype(jnp.bfloat16))


def with_collectives(
    hidden,
    input_norm_gain,
    query_weight,
    key_value_weight,
    adapter_down_weight,
    adapter_up_weight,
    key_value_cache,
    valid_cache_lengths,
    request_per_slot,
    slot_per_request,
):
    owner_index = lax.axis_index("adapter")
    device_slots = lax.dynamic_slice_in_dim(request_per_slot, owner_index * ADP_DEV, ADP_DEV, 0)
    normed = rms_norm(hidden, input_norm_gain)
    query_steps = []
    keyvalue_steps = []
    for step_index in range(2):
        block_of_rows = lax.all_gather(normed[step_index], "adapter", axis=0, tiled=True)
        device_query, keyvalue_local = project_input(
            block_of_rows,
            query_weight,
            key_value_weight,
            adapter_down_weight,
            adapter_up_weight,
            device_slots,
            slot_per_request,
        )
        query_row_list, key_value_rows = (
            lax.all_to_all(device_query, "adapter", split_axis=0, concat_axis=1, tiled=True),
            lax.all_to_all(keyvalue_local, "adapter", split_axis=0, concat_axis=1, tiled=True),
        )
        query_steps.append(query_row_list)
        keyvalue_steps.append(key_value_rows)
    results = []
    fresh_keys_list = []
    latest_value_list = []
    for step_index in range(2):
        query_row_list = query_steps[step_index]
        key_value_rows = keyvalue_steps[step_index]
        token_positions = valid_cache_lengths + step_index
        rotated_query = apply_rotation(
            query_row_list.astype(jnp.float32), token_positions, QUERY_HEADS
        ).astype(jnp.bfloat16)
        incoming_key = apply_rotation(
            key_value_rows[:, : KEY_VALUE_HEADS * HEAD_SIZE].astype(jnp.float32),
            token_positions,
            KEY_VALUE_HEADS,
        ).astype(jnp.bfloat16)
        fresh_keys_list.append(incoming_key)
        latest_value_list.append(key_value_rows[:, KEY_VALUE_HEADS * HEAD_SIZE :])
        results.append(
            attend(
                rotated_query,
                key_value_cache,
                valid_cache_lengths,
                jnp.stack(fresh_keys_list, axis=1),
                jnp.stack(latest_value_list, axis=1),
            )
        )
    return jnp.stack(results)


MESH = pl.DeviceIdType.MESH
F32 = jnp.float32
BF16 = jnp.bfloat16


def block_kernel(
    parties,
    capacity,
    hidden_ref,
    gain_ref,
    query_weight_ref,
    key_value_weight_ref,
    down_ref,
    up_ref,
    cache_ref,
    length_source,
    request_of_source,
    slot_of_source,
    out_ref,
    length_ref,
    request_of_ref,
    slot_of_ref,
    hidden,
    gain,
    query_weight,
    key_value_weight,
    down,
    up,
    keys,
    values,
    gathered,
    spread_rows,
    rows,
    staged,
    ranks,
    pair_rows,
    pair_send,
    pair_received,
    result,
    local_sem,
    gather_send_sem,
    gather_sem,
    forward_send_sem,
    rank_send_sem,
    rank_sem,
    pair_send_sem,
    pair_sem,
):
    n = parties
    chips = n // 2
    width = rows.shape[1]
    blocks = width // HEAD_SIZE
    heads = query_weight.shape[1] // HEAD_SIZE
    total = keys.shape[0]
    me = lax.axis_index("adapter")
    core = lax.rem(me, 2)
    chip = me // 2
    sibling = chip * 2 + 1 - core
    bits = n.bit_length() - 1
    steps_of_bit = [(1 - 2 * ((me // 2 ** b) % 2)) * 2 ** b for b in range(bits)]

    def partner(mask):
        other = me
        for b in range(bits):
            if mask // 2 ** b % 2:
                other = other + steps_of_bit[b]
        return other


    loads = [
        (down_ref, down),
        (query_weight_ref, query_weight),
        (key_value_weight_ref, key_value_weight),
        (up_ref, up),
        (cache_ref.at[0, 0], keys.at[pl.ds(0, capacity)]),
        (cache_ref.at[0, 1], values.at[pl.ds(0, capacity)]),
        (hidden_ref, hidden),
        (gain_ref, gain),
        (length_source, length_ref),
        (request_of_source, request_of_ref),
        (slot_of_source, slot_of_ref),
    ]
    copies = [
        pltpu.make_async_copy(source, target, local_sem.at[number])
        for number, (source, target) in enumerate(loads)
    ]

    for copy in copies[6:]:
        copy.start()
    barrier = pltpu.get_barrier_semaphore()

    for mask in reversed(range(1, n)):
        pl.semaphore_signal(
            barrier, inc=1, device_id={"adapter": partner(mask)}, device_id_type=MESH
        )
    for copy in copies[:6]:
        copy.start()
    copies[6].wait()
    copies[7].wait()

    for block in range(blocks):
        piece = hidden[:, block * HEAD_SIZE : (block + 1) * HEAD_SIZE].astype(F32)
        for step in range(2):
            staged[pl.ds(step * blocks + block, 1), :] = piece[step : step + 1]
    for step in range(2):
        part = staged[step * blocks : (step + 1) * blocks, :]
        squares = jnp.sum(jnp.sum(part * part, axis=0, keepdims=True), axis=1, keepdims=True)
        part = part * lax.rsqrt(squares * (1.0 / width) + 1e-05) * gain[...]
        gathered[me, step * blocks : (step + 1) * blocks, :] = part.astype(BF16)

    tail = total - capacity
    keys[capacity:, :] = jnp.zeros((tail, keys.shape[1]), BF16)
    values[capacity:, :] = jnp.zeros((tail, values.shape[1]), BF16)

    pl.semaphore_wait(barrier, n - 1)

    def own_copy(k, target):
        return pltpu.make_async_remote_copy(
            src_ref=gathered.at[me],
            dst_ref=gathered.at[me],
            send_sem=gather_send_sem.at[k],
            recv_sem=gather_sem.at[me],
            device_id={"adapter": target},
            device_id_type=MESH,
        )

    def sibling_copy(source):
        return pltpu.make_async_remote_copy(
            src_ref=gathered.at[source],
            dst_ref=gathered.at[source],
            send_sem=forward_send_sem.at[source // 2],
            recv_sem=gather_sem.at[source],
            device_id={"adapter": sibling},
            device_id_type=MESH,
        )

    across = 1
    far = chips - 2
    passed_on = range(2, far, 2)
    straight = [k for k in reversed(passed_on)] + [far + across, far, across]
    for k in straight:
        own_copy(k, partner(2 * k)).start()
        if k == passed_on[0]:
            for first in passed_on:
                own_copy(first, sibling).wait_send()
    sibling_copy(me).start()

    def place(source):
        spread_rows[pl.ds(source, 2 * blocks, stride=n), :] = gathered[source].astype(F32)

    for copy in copies[8:]:
        copy.wait()
    length = length_ref[0]
    row_index = lax.broadcasted_iota(jnp.int32, (24, HEAD_SIZE), 0)
    lane_index = lax.broadcasted_iota(jnp.int32, (24, HEAD_SIZE), 1)
    half = HEAD_SIZE // 2
    step_of_row = jnp.where(row_index < 16, (row_index // heads) % 2, row_index % 2)
    turn = (lane_index % half).astype(F32) * (-1.0 / half)
    frequency = jnp.exp(turn * math.log(ROPE_BASE))
    angles = (step_of_row + length).astype(F32) * frequency
    cosine = jnp.cos(angles)
    sine = jnp.sin(angles)
    sine = jnp.where(lane_index < half, -sine, sine)

    request_rows = lax.broadcasted_iota(jnp.int32, (n, HEAD_SIZE), 0)
    adapter_of = jnp.zeros((n, HEAD_SIZE), jnp.int32)
    for request in range(n):
        adapter_of = jnp.where(request_rows == request, slot_of_ref[request] // 2, adapter_of)
    mine = (request_rows == request_of_ref[0, me]) | (request_rows == request_of_ref[1, me])

    place(me)

    def arrival(k):
        source = partner(2 * k)
        pltpu.make_async_remote_copy(
            src_ref=gathered.at[source],
            dst_ref=gathered.at[source],
            send_sem=gather_send_sem.at[0],
            recv_sem=gather_sem.at[source],
            device_id={"adapter": sibling},
            device_id_type=MESH,
        ).wait_recv()
        return source

    def across_copy(k):
        source = partner(2 * k)
        return pltpu.make_async_remote_copy(
            src_ref=gathered.at[source],
            dst_ref=gathered.at[source],
            send_sem=gather_send_sem.at[k + across],
            recv_sem=gather_sem.at[source],
            device_id={"adapter": partner(2 * across)},
            device_id_type=MESH,
        )

    for k in passed_on:
        source = arrival(k)
        across_copy(k).start()
        sibling_copy(source).start()
    for k in passed_on:
        place(partner(2 * k))
    for k in [across] + [k + across for k in passed_on if k != far - 2] + [
        far,
        far + across,
        far - 2 + across,
    ]:
        source = arrival(k)
        sibling_copy(source).start()
        place(source)

    for k in range(chips):
        source = partner(2 * k + 1)
        sibling_copy(source).wait_recv()
        place(source)

    copies[0].wait()
    chunk = 4096
    per_chunk = chunk // HEAD_SIZE

    def shrink(c, acc):
        pieces = []
        for step in range(2):
            line = []
            for b in range(per_chunk):
                start = pl.multiple_of((step * blocks + c * per_chunk + b) * n, n)
                line.append(spread_rows[pl.ds(start, n), :].astype(BF16))
            pieces.append(jnp.concatenate(line, axis=1))
        piece = jnp.concatenate(pieces, axis=0)
        columns = pl.ds(pl.multiple_of(c * chunk, chunk), chunk)
        rows[:, columns] = piece
        return acc + lax.dot_general(
            piece, down[:, columns], (((1,), (1,)), ((), ())), preferred_element_type=F32
        )

    shrunk = lax.fori_loop(
        0, width // chunk, shrink, jnp.zeros((2 * n, ADAPTER_RANK), F32)
    )
    rank_lanes = lax.broadcasted_iota(jnp.int32, (n, HEAD_SIZE), 1)
    message = jnp.concatenate([shrunk[:n], shrunk[n:]], axis=1)
    ranks[me] = jnp.where(mine, message, 0.0).astype(BF16)

    def rank_copy(k, target):
        return pltpu.make_async_remote_copy(
            src_ref=ranks.at[me],
            dst_ref=ranks.at[me],
            send_sem=rank_send_sem.at[k],
            recv_sem=rank_sem.at[me],
            device_id={"adapter": target},
            device_id_type=MESH,
        )

    for mask in reversed(range(1, n)):
        rank_copy(mask, partner(mask)).start()

    copies[1].wait()
    copies[2].wait()

    def project(c, carry):
        query, keyvalue = carry
        columns = pl.ds(pl.multiple_of(c * chunk, chunk), chunk)
        piece = rows[:, columns]
        query = query + jnp.dot(piece, query_weight[columns, :], preferred_element_type=F32)
        keyvalue = keyvalue + jnp.dot(
            piece, key_value_weight[columns, :], preferred_element_type=F32
        )
        return query, keyvalue

    query, keyvalue = lax.fori_loop(
        0,
        width // chunk,
        project,
        (jnp.zeros((2 * n, query_weight.shape[1]), F32), jnp.zeros((2 * n, HEAD_SIZE), F32)),
    )
    for step in range(2):
        pair_rows[pl.ds(2 * heads + step, n, stride=16), :] = keyvalue[step * n : (step + 1) * n]

    copies[3].wait()

    def rank_arrival(k, carry):
        source = lax.rem(me + n - k, n)
        pltpu.make_async_remote_copy(
            src_ref=ranks.at[source],
            dst_ref=ranks.at[source],
            send_sem=rank_send_sem.at[0],
            recv_sem=rank_sem.at[source],
            device_id={"adapter": source},
            device_id_type=MESH,
        ).wait_recv()
        return carry

    lax.fori_loop(1, n, rank_arrival, 0)
    ranked = ranks[0].astype(F32)
    for source in range(1, n):
        ranked = ranked + ranks[source].astype(F32)
    turned = pltpu.roll(ranked, ADAPTER_RANK, 1)
    low = rank_lanes < ADAPTER_RANK
    both = jnp.concatenate(
        [jnp.where(low, ranked, turned), jnp.where(low, turned, ranked)], axis=0
    )
    adapter_rows = jnp.concatenate([adapter_of, adapter_of], axis=0)
    lane_half = lax.broadcasted_iota(jnp.int32, (2 * n, HEAD_SIZE), 1) // ADAPTER_RANK
    masked = [
        jnp.where(adapter_rows == 2 * pair + lane_half, both, 0.0).astype(BF16)
        for pair in range(n // 2)
    ]
    delta = jnp.dot(jnp.concatenate(masked, axis=1), up[...], preferred_element_type=F32)
    query = query + ADAPTER_SCALE * delta
    for step in range(2):
        for head in range(heads):
            pair_rows[pl.ds(step * heads + head, n, stride=16), :] = query[
                step * n : (step + 1) * n, head * HEAD_SIZE : (head + 1) * HEAD_SIZE
            ]
    for request in range(n):
        pair_send[request] = pair_rows[request * 16 : (request + 1) * 16, :].astype(BF16)

    def pair_copy(k, target):
        return pltpu.make_async_remote_copy(
            src_ref=pair_send.at[target],
            dst_ref=pair_received.at[me],
            send_sem=pair_send_sem.at[k],
            recv_sem=pair_sem.at[me],
            device_id={"adapter": target},
            device_id_type=MESH,
        )

    for mask in reversed(range(1, n)):
        pair_copy(mask, partner(mask)).start()
    pair_received[me] = pair_send[me]

    copies[4].wait()
    copies[5].wait()

    def finish_ranks(k, carry):
        rank_copy(k, sibling).wait_send()
        return carry

    lax.fori_loop(1, n, finish_ranks, 0)

    for k in straight[len(passed_on) :]:
        own_copy(k, sibling).wait_send()
    for k in passed_on:
        across_copy(k).wait_send()

    def finish_forward(k, carry):
        sibling_copy(2 * k + core).wait_send()
        return carry

    lax.fori_loop(0, chips, finish_forward, 0)

    def pair_arrival(k, carry):
        source = lax.rem(me + n - k, n)
        pltpu.make_async_remote_copy(
            src_ref=pair_send.at[source],
            dst_ref=pair_received.at[source],
            send_sem=pair_send_sem.at[0],
            recv_sem=pair_sem.at[source],
            device_id={"adapter": source},
            device_id_type=MESH,
        ).wait_recv()
        return carry

    lax.fori_loop(1, n, pair_arrival, 0)

    columns = lax.broadcasted_iota(jnp.int32, (16, total), 1)
    steps = (lax.broadcasted_iota(jnp.int32, (16, total), 0) // heads) % 2
    valid = (columns < length) | ((columns >= capacity) & (columns - capacity <= steps))
    fresh = lax.broadcasted_iota(jnp.int32, (8, HEAD_SIZE), 0) < 2
    padding = jnp.zeros((8, HEAD_SIZE), F32)
    turned_queries = []
    for group in range(KEY_VALUE_HEADS):
        turned_query = jnp.concatenate(
            [
                pair_received[2 * group].astype(F32)[:8],
                pair_received[2 * group + 1].astype(F32)[:8],
            ],
            axis=0,
        )
        turned_query = turned_query * cosine[:16] + pltpu.roll(turned_query, half, 1) * sine[:16]
        turned_queries.append(turned_query.astype(BF16))
    new_keys = []
    new_values = []
    for group in range(KEY_VALUE_HEADS):
        key = pair_received[group].astype(F32)[8:]
        key = key * cosine[16:] + pltpu.roll(key, half, 1) * sine[16:]
        key = jnp.concatenate([jnp.where(fresh, key, 0.0), padding], axis=0)
        new_keys.append(key.astype(BF16))
        value = pair_received[KEY_VALUE_HEADS + group].astype(F32)[8:]
        value = jnp.concatenate([jnp.where(fresh, value, 0.0), padding], axis=0)
        new_values.append(value.astype(BF16))
    keys[capacity : capacity + 16, :] = jnp.concatenate(new_keys, axis=1)
    values[capacity : capacity + 16, :] = jnp.concatenate(new_values, axis=1)
    scores = [
        lax.dot_general(
            turned_queries[group],
            keys[:, group * HEAD_SIZE : (group + 1) * HEAD_SIZE],
            (((1,), (1,)), ((), ())),
            preferred_element_type=F32,
        )
        for group in range(KEY_VALUE_HEADS)
    ]
    scores = [jnp.where(valid, part * HEAD_SIZE ** (-0.5), -1e30) for part in scores]
    tops = [jnp.max(part, axis=1, keepdims=True) for part in scores]
    weights = [
        jnp.where(valid, jnp.exp(part - top), 0.0) for part, top in zip(scores, tops)
    ]
    sums = [jnp.sum(part, axis=1, keepdims=True) for part in weights]
    weights = [(part / whole).astype(BF16) for part, whole in zip(weights, sums)]
    mixed = [
        jnp.dot(
            weights[group],
            values[:, group * HEAD_SIZE : (group + 1) * HEAD_SIZE],
            preferred_element_type=F32,
        )
        for group in range(KEY_VALUE_HEADS)
    ]
    for group in range(KEY_VALUE_HEADS):
        for side in range(2):
            for step in range(2):
                for head in range(heads):
                    start = ((2 * group + side) * heads + head) * HEAD_SIZE
                    line = (side * 2 + step) * heads + head
                    result[step : step + 1, start : start + HEAD_SIZE] = mixed[group][
                        line : line + 1
                    ]
    out_ref[...] = result[...].astype(BF16)

    def finish(k, carry):
        pair_copy(k, sibling).wait_send()
        return carry

    lax.fori_loop(1, n, finish, 0)


def whole_block(
    hidden,
    input_norm_gain,
    query_weight,
    key_value_weight,
    adapter_down_weight,
    adapter_up_weight,
    key_value_cache,
    valid_cache_lengths,
    request_per_slot,
    slot_per_request,
):
    n = request_per_slot.shape[0]
    width = hidden.shape[2]
    blocks = width // HEAD_SIZE
    capacity = key_value_cache.shape[2]
    kv_width = key_value_cache.shape[3]
    total = capacity + HEAD_SIZE
    columns = query_weight.shape[1]
    in_hbm = pl.BlockSpec(memory_space=pltpu.HBM)
    in_vmem = pl.BlockSpec(memory_space=pltpu.VMEM)
    dma = pltpu.SemaphoreType.DMA
    call = pl.pallas_call(
        functools.partial(block_kernel, n, capacity),
        out_shape=jax.ShapeDtypeStruct((2, width), BF16),
        in_specs=[in_hbm] * 10,
        out_specs=in_vmem,
        scratch_shapes=[
            pltpu.SMEM(valid_cache_lengths.shape, jnp.int32),
            pltpu.SMEM(request_per_slot.shape[::-1], jnp.int32),
            pltpu.SMEM(slot_per_request.shape, jnp.int32),
            pltpu.VMEM((2, width), BF16),
            pltpu.VMEM((blocks, HEAD_SIZE), F32),
            pltpu.VMEM((width, columns), BF16),
            pltpu.VMEM((width, HEAD_SIZE), BF16),
            pltpu.VMEM((ADAPTER_RANK, width), BF16),
            pltpu.VMEM((n * ADAPTER_RANK, columns), BF16),
            pltpu.VMEM((total, kv_width), BF16),
            pltpu.VMEM((total, kv_width), BF16),
            pltpu.VMEM((n, 2 * blocks, HEAD_SIZE), BF16),
            pltpu.VMEM((2 * blocks * n, HEAD_SIZE), F32),
            pltpu.VMEM((2 * n, width), BF16),
            pltpu.VMEM((2 * blocks, HEAD_SIZE), F32),
            pltpu.VMEM((n, n, HEAD_SIZE), BF16),
            pltpu.VMEM((n * 16, HEAD_SIZE), F32),
            pltpu.VMEM((n, 16, HEAD_SIZE), BF16),
            pltpu.VMEM((n, 16, HEAD_SIZE), BF16),
            pltpu.VMEM((2, width), F32),
            dma((11,)),
            dma((n // 2,)),
            dma((n,)),
            dma((n // 2,)),
            dma((n,)),
            dma((n,)),
            dma((n,)),
            dma((n,)),
        ],
        compiler_params=pltpu.CompilerParams(
            collective_id=0, has_side_effects=True, vmem_limit_bytes=63 * 2 ** 20
        ),
        name="decode_block",
    )
    out = call(
        hidden.reshape(2, width),
        input_norm_gain.reshape(blocks, HEAD_SIZE),
        query_weight,
        key_value_weight,
        adapter_down_weight.reshape(ADAPTER_RANK, width),
        adapter_up_weight.reshape(n * ADAPTER_RANK, columns),
        key_value_cache,
        valid_cache_lengths,
        request_per_slot.T,
        slot_per_request,
    )
    return out.reshape(2, 1, width)


def on_device(*arguments):
    hidden, _, query_weight, key_value_weight, _, _, _, _, request_per_slot, _ = arguments
    fits = (
        hidden.shape[1] == 1
        and key_value_weight.shape[1] == HEAD_SIZE
        and query_weight.shape[1] == 4 * HEAD_SIZE
        and request_per_slot.shape[0] == 16
    )
    return whole_block(*arguments) if fits else with_collectives(*arguments)


def solution(mesh):
    in_specs = (
        P(None, ("replica", "adapter"), None),
        P(),
        P(None, "adapter"),
        P(None, "adapter"),
        P(("replica", "adapter"), None, None),
        P("replica", None, "adapter"),
        P(("replica", "adapter"), None, None, None),
        P(("replica", "adapter")),
        P("replica", None),
        P("replica"),
    )
    out_specs = P(None, ("replica", "adapter"), None)
    return jax.shard_map(
        on_device, mesh=mesh, in_specs=in_specs, out_specs=out_specs, check_vma=False
    )
```

```python
import functools
import math

import jax
import jax.numpy as jnp
from jax import lax
from jax.experimental import pallas as pl
from jax.experimental.pallas import tpu as pltpu
from jax.sharding import PartitionSpec as P

QUERY_HEADS = 64
KEY_VALUE_HEADS = 8
HEAD_SIZE = 128
ADP_DEV = 1
ADAPTER_RANK = 64


ADAPTER_SCALE = 0.5
ROPE_BASE = 500000.0


def rms_norm(hidden_rows, input_norm_gain):
    values = hidden_rows.astype(jnp.float32)
    spread = jnp.mean(values * values, axis=-1, keepdims=True)
    return (values * lax.rsqrt(spread + 1e-05) * input_norm_gain).astype(jnp.bfloat16)


def apply_rotation(values, token_positions, heads):
    batch_row_list = values.shape[0]
    shaped = values.reshape(batch_row_list, heads, -1)
    half_dim = shaped.shape[-1] // 2
    frequency = ROPE_BASE ** (-jnp.arange(half_dim, dtype=jnp.float32) / half_dim)
    angles = token_positions.astype(jnp.float32)[:, None, None] * frequency[None, None, :]
    cosine = jnp.cos(angles)
    sine_part = jnp.sin(angles)
    first = shaped[..., :half_dim]
    second = shaped[..., half_dim:]
    turned = jnp.concatenate(
        [first * cosine - second * sine_part, second * cosine + first * sine_part], axis=-1
    )
    return turned.reshape(batch_row_list, -1)


def attend(query_row_list, block_of_cache, lengths, latest_keys, latest_values):
    batch_row_list = query_row_list.shape[0]
    query_matrix = query_row_list.reshape(
        batch_row_list, KEY_VALUE_HEADS, QUERY_HEADS // KEY_VALUE_HEADS, HEAD_SIZE
    )
    cached_key_rows = block_of_cache[:, 0].reshape(batch_row_list, -1, KEY_VALUE_HEADS, HEAD_SIZE)
    cached_value_rows = block_of_cache[:, 1].reshape(batch_row_list, -1, KEY_VALUE_HEADS, HEAD_SIZE)
    appended_keys = latest_keys.reshape(batch_row_list, -1, KEY_VALUE_HEADS, HEAD_SIZE)
    appended_values = latest_values.reshape(batch_row_list, -1, KEY_VALUE_HEADS, HEAD_SIZE)
    score_scale = HEAD_SIZE ** (-0.5)
    old_scores = (
        jnp.einsum(
            "bhgd,blhd->bhgl", query_matrix, cached_key_rows, preferred_element_type=jnp.float32
        )
        * score_scale
    )
    valid_mask = (jnp.arange(cached_key_rows.shape[1])[None, :] < lengths[:, None])[
        :, None, None, :
    ]
    old_scores = jnp.where(valid_mask, old_scores, -1e30)
    new_scores = (
        jnp.einsum(
            "bhgd,bshd->bhgs", query_matrix, appended_keys, preferred_element_type=jnp.float32
        )
        * score_scale
    )
    row_top = jnp.maximum(jnp.max(old_scores, axis=-1), jnp.max(new_scores, axis=-1))[..., None]
    old_weights = jnp.where(valid_mask, jnp.exp(old_scores - row_top), 0.0)
    new_weights = jnp.exp(new_scores - row_top)
    weight_total = jnp.sum(old_weights, axis=-1, keepdims=True) + jnp.sum(
        new_weights, axis=-1, keepdims=True
    )
    old_probs = (old_weights / weight_total).astype(jnp.bfloat16)
    new_probs = (new_weights / weight_total).astype(jnp.bfloat16)
    mixed = jnp.einsum(
        "bhgl,blhd->bhgd", old_probs, cached_value_rows, preferred_element_type=jnp.float32
    )
    mixed = mixed + jnp.einsum(
        "bhgs,bshd->bhgd", new_probs, appended_values, preferred_element_type=jnp.float32
    )
    return mixed.reshape(batch_row_list, -1).astype(jnp.bfloat16)


def project_input(
    block_of_rows,
    query_weight,
    key_value_weight,
    adapter_down_weight,
    adapter_up_weight,
    device_slots,
    slot_per_request,
):
    base_query = jnp.dot(block_of_rows, query_weight, preferred_element_type=jnp.float32)
    base_kv = jnp.dot(block_of_rows, key_value_weight, preferred_element_type=jnp.float32)
    padded = jnp.concatenate(
        [block_of_rows, jnp.zeros((1, block_of_rows.shape[1]), jnp.bfloat16)], axis=0
    )
    selected_rows = padded[device_slots]
    reduced_rows = jnp.einsum(
        "hmb,hgb->hmg", selected_rows, adapter_down_weight, preferred_element_type=jnp.float32
    ).astype(jnp.bfloat16)
    every_slot = lax.all_gather(reduced_rows, "adapter", axis=0, tiled=True)
    slot_contributions = jnp.einsum(
        "qzf,qfo->qzo", every_slot, adapter_up_weight, preferred_element_type=jnp.float32
    )
    adapter_delta = slot_contributions.reshape(-1, adapter_up_weight.shape[2])[slot_per_request]
    device_query = (base_query + ADAPTER_SCALE * adapter_delta).astype(jnp.bfloat16)
    return (device_query, base_kv.astype(jnp.bfloat16))


def with_collectives(
    hidden,
    input_norm_gain,
    query_weight,
    key_value_weight,
    adapter_down_weight,
    adapter_up_weight,
    key_value_cache,
    valid_cache_lengths,
    request_per_slot,
    slot_per_request,
):
    owner_index = lax.axis_index("adapter")
    device_slots = lax.dynamic_slice_in_dim(request_per_slot, owner_index * ADP_DEV, ADP_DEV, 0)
    normed = rms_norm(hidden, input_norm_gain)
    query_steps = []
    keyvalue_steps = []
    for step_index in range(2):
        block_of_rows = lax.all_gather(normed[step_index], "adapter", axis=0, tiled=True)
        device_query, keyvalue_local = project_input(
            block_of_rows,
            query_weight,
            key_value_weight,
            adapter_down_weight,
            adapter_up_weight,
            device_slots,
            slot_per_request,
        )
        query_row_list, key_value_rows = (
            lax.all_to_all(device_query, "adapter", split_axis=0, concat_axis=1, tiled=True),
            lax.all_to_all(keyvalue_local, "adapter", split_axis=0, concat_axis=1, tiled=True),
        )
        query_steps.append(query_row_list)
        keyvalue_steps.append(key_value_rows)
    results = []
    fresh_keys_list = []
    latest_value_list = []
    for step_index in range(2):
        query_row_list = query_steps[step_index]
        key_value_rows = keyvalue_steps[step_index]
        token_positions = valid_cache_lengths + step_index
        rotated_query = apply_rotation(
            query_row_list.astype(jnp.float32), token_positions, QUERY_HEADS
        ).astype(jnp.bfloat16)
        incoming_key = apply_rotation(
            key_value_rows[:, : KEY_VALUE_HEADS * HEAD_SIZE].astype(jnp.float32),
            token_positions,
            KEY_VALUE_HEADS,
        ).astype(jnp.bfloat16)
        fresh_keys_list.append(incoming_key)
        latest_value_list.append(key_value_rows[:, KEY_VALUE_HEADS * HEAD_SIZE :])
        results.append(
            attend(
                rotated_query,
                key_value_cache,
                valid_cache_lengths,
                jnp.stack(fresh_keys_list, axis=1),
                jnp.stack(latest_value_list, axis=1),
            )
        )
    return jnp.stack(results)


MESH = pl.DeviceIdType.MESH
F32 = jnp.float32
BF16 = jnp.bfloat16


def block_kernel(
    parties,
    capacity,
    hidden_ref,
    gain_ref,
    query_weight_ref,
    key_value_weight_ref,
    down_ref,
    up_ref,
    cache_ref,
    length_source,
    request_of_source,
    slot_of_source,
    out_ref,
    length_ref,
    request_of_ref,
    slot_of_ref,
    hidden,
    gain,
    query_weight,
    key_value_weight,
    down,
    up,
    keys,
    values,
    gathered,
    spread_rows,
    rows,
    staged,
    ranks,
    pair_rows,
    pair_send,
    pair_received,
    result,
    local_sem,
    gather_send_sem,
    gather_sem,
    forward_send_sem,
    rank_send_sem,
    rank_sem,
    pair_send_sem,
    pair_sem,
):
    n = parties
    chips = n // 2
    width = rows.shape[1]
    blocks = width // HEAD_SIZE
    heads = query_weight.shape[1] // HEAD_SIZE
    total = keys.shape[0]
    me = lax.axis_index("adapter")
    core = lax.rem(me, 2)
    chip = me // 2
    sibling = chip * 2 + 1 - core
    bits = n.bit_length() - 1
    steps_of_bit = [(1 - 2 * ((me // 2 ** b) % 2)) * 2 ** b for b in range(bits)]

    def partner(mask):
        other = me
        for b in range(bits):
            if mask // 2 ** b % 2:
                other = other + steps_of_bit[b]
        return other


    loads = [
        (down_ref, down),
        (query_weight_ref, query_weight),
        (key_value_weight_ref, key_value_weight),
        (up_ref, up),
        (cache_ref.at[0, 0], keys.at[pl.ds(0, capacity)]),
        (cache_ref.at[0, 1], values.at[pl.ds(0, capacity)]),
        (hidden_ref, hidden),
        (gain_ref, gain),
        (length_source, length_ref),
        (request_of_source, request_of_ref),
        (slot_of_source, slot_of_ref),
    ]
    copies = [
        pltpu.make_async_copy(source, target, local_sem.at[number])
        for number, (source, target) in enumerate(loads)
    ]

    for copy in copies[6:]:
        copy.start()
    barrier = pltpu.get_barrier_semaphore()

    for mask in reversed(range(1, n)):
        pl.semaphore_signal(
            barrier, inc=1, device_id={"adapter": partner(mask)}, device_id_type=MESH
        )
    for copy in copies[:6]:
        copy.start()
    copies[6].wait()
    copies[7].wait()

    for block in range(blocks):
        piece = hidden[:, block * HEAD_SIZE : (block + 1) * HEAD_SIZE].astype(F32)
        for step in range(2):
            staged[pl.ds(step * blocks + block, 1), :] = piece[step : step + 1]
    for step in range(2):
        part = staged[step * blocks : (step + 1) * blocks, :]
        squares = jnp.sum(jnp.sum(part * part, axis=0, keepdims=True), axis=1, keepdims=True)
        part = part * lax.rsqrt(squares * (1.0 / width) + 1e-05) * gain[...]
        gathered[me, step * blocks : (step + 1) * blocks, :] = part.astype(BF16)

    tail = total - capacity
    keys[capacity:, :] = jnp.zeros((tail, keys.shape[1]), BF16)
    values[capacity:, :] = jnp.zeros((tail, values.shape[1]), BF16)

    pl.semaphore_wait(barrier, n - 1)

    def own_copy(k, target):
        return pltpu.make_async_remote_copy(
            src_ref=gathered.at[me],
            dst_ref=gathered.at[me],
            send_sem=gather_send_sem.at[k],
            recv_sem=gather_sem.at[me],
            device_id={"adapter": target},
            device_id_type=MESH,
        )

    def sibling_copy(source):
        return pltpu.make_async_remote_copy(
            src_ref=gathered.at[source],
            dst_ref=gathered.at[source],
            send_sem=forward_send_sem.at[source // 2],
            recv_sem=gather_sem.at[source],
            device_id={"adapter": sibling},
            device_id_type=MESH,
        )

    across = 1
    far = chips - 2
    passed_on = range(2, far, 2)
    straight = [across] + [k for k in reversed(passed_on)] + [far + across, far]
    for k in straight:
        own_copy(k, partner(2 * k)).start()
        if k == passed_on[0]:
            for first in passed_on:
                own_copy(first, sibling).wait_send()
    sibling_copy(me).start()

    def place(source):
        spread_rows[pl.ds(source, 2 * blocks, stride=n), :] = gathered[source].astype(F32)

    for copy in copies[8:]:
        copy.wait()
    length = length_ref[0]
    row_index = lax.broadcasted_iota(jnp.int32, (24, HEAD_SIZE), 0)
    lane_index = lax.broadcasted_iota(jnp.int32, (24, HEAD_SIZE), 1)
    half = HEAD_SIZE // 2
    step_of_row = jnp.where(row_index < 16, (row_index // heads) % 2, row_index % 2)
    turn = (lane_index % half).astype(F32) * (-1.0 / half)
    frequency = jnp.exp(turn * math.log(ROPE_BASE))
    angles = (step_of_row + length).astype(F32) * frequency
    cosine = jnp.cos(angles)
    sine = jnp.sin(angles)
    sine = jnp.where(lane_index < half, -sine, sine)

    request_rows = lax.broadcasted_iota(jnp.int32, (n, HEAD_SIZE), 0)
    adapter_of = jnp.zeros((n, HEAD_SIZE), jnp.int32)
    for request in range(n):
        adapter_of = jnp.where(request_rows == request, slot_of_ref[request] // 2, adapter_of)
    mine = (request_rows == request_of_ref[0, me]) | (request_rows == request_of_ref[1, me])

    place(me)

    def arrival(k):
        source = partner(2 * k)
        pltpu.make_async_remote_copy(
            src_ref=gathered.at[source],
            dst_ref=gathered.at[source],
            send_sem=gather_send_sem.at[0],
            recv_sem=gather_sem.at[source],
            device_id={"adapter": sibling},
            device_id_type=MESH,
        ).wait_recv()
        return source

    def across_copy(k):
        source = partner(2 * k)
        return pltpu.make_async_remote_copy(
            src_ref=gathered.at[source],
            dst_ref=gathered.at[source],
            send_sem=gather_send_sem.at[k + across],
            recv_sem=gather_sem.at[source],
            device_id={"adapter": partner(2 * across)},
            device_id_type=MESH,
        )

    for k in passed_on:
        source = arrival(k)
        across_copy(k).start()
        sibling_copy(source).start()
    for k in passed_on:
        place(partner(2 * k))
    for k in [across] + [k + across for k in passed_on if k != far - 2] + [
        far,
        far + across,
        far - 2 + across,
    ]:
        source = arrival(k)
        sibling_copy(source).start()
        place(source)

    for k in range(chips):
        source = partner(2 * k + 1)
        sibling_copy(source).wait_recv()
        place(source)

    copies[0].wait()
    chunk = 4096
    per_chunk = chunk // HEAD_SIZE

    def shrink(c, acc):
        pieces = []
        for step in range(2):
            line = []
            for b in range(per_chunk):
                start = pl.multiple_of((step * blocks + c * per_chunk + b) * n, n)
                line.append(spread_rows[pl.ds(start, n), :].astype(BF16))
            pieces.append(jnp.concatenate(line, axis=1))
        piece = jnp.concatenate(pieces, axis=0)
        columns = pl.ds(pl.multiple_of(c * chunk, chunk), chunk)
        rows[:, columns] = piece
        return acc + lax.dot_general(
            piece, down[:, columns], (((1,), (1,)), ((), ())), preferred_element_type=F32
        )

    shrunk = lax.fori_loop(
        0, width // chunk, shrink, jnp.zeros((2 * n, ADAPTER_RANK), F32)
    )
    rank_lanes = lax.broadcasted_iota(jnp.int32, (n, HEAD_SIZE), 1)
    message = jnp.concatenate([shrunk[:n], shrunk[n:]], axis=1)
    ranks[me] = jnp.where(mine, message, 0.0).astype(BF16)

    def rank_copy(k, target):
        return pltpu.make_async_remote_copy(
            src_ref=ranks.at[me],
            dst_ref=ranks.at[me],
            send_sem=rank_send_sem.at[k],
            recv_sem=rank_sem.at[me],
            device_id={"adapter": target},
            device_id_type=MESH,
        )

    for mask in reversed(range(1, n)):
        rank_copy(mask, partner(mask)).start()

    copies[1].wait()
    copies[2].wait()

    def project(c, carry):
        query, keyvalue = carry
        columns = pl.ds(pl.multiple_of(c * chunk, chunk), chunk)
        piece = rows[:, columns]
        query = query + jnp.dot(piece, query_weight[columns, :], preferred_element_type=F32)
        keyvalue = keyvalue + jnp.dot(
            piece, key_value_weight[columns, :], preferred_element_type=F32
        )
        return query, keyvalue

    query, keyvalue = lax.fori_loop(
        0,
        width // chunk,
        project,
        (jnp.zeros((2 * n, query_weight.shape[1]), F32), jnp.zeros((2 * n, HEAD_SIZE), F32)),
    )
    for step in range(2):
        pair_rows[pl.ds(2 * heads + step, n, stride=16), :] = keyvalue[step * n : (step + 1) * n]

    copies[3].wait()

    def rank_arrival(k, carry):
        source = lax.rem(me + n - k, n)
        pltpu.make_async_remote_copy(
            src_ref=ranks.at[source],
            dst_ref=ranks.at[source],
            send_sem=rank_send_sem.at[0],
            recv_sem=rank_sem.at[source],
            device_id={"adapter": source},
            device_id_type=MESH,
        ).wait_recv()
        return carry

    lax.fori_loop(1, n, rank_arrival, 0)
    ranked = ranks[0].astype(F32)
    for source in range(1, n):
        ranked = ranked + ranks[source].astype(F32)
    turned = pltpu.roll(ranked, ADAPTER_RANK, 1)
    low = rank_lanes < ADAPTER_RANK
    both = jnp.concatenate(
        [jnp.where(low, ranked, turned), jnp.where(low, turned, ranked)], axis=0
    )
    adapter_rows = jnp.concatenate([adapter_of, adapter_of], axis=0)
    lane_half = lax.broadcasted_iota(jnp.int32, (2 * n, HEAD_SIZE), 1) // ADAPTER_RANK
    masked = [
        jnp.where(adapter_rows == 2 * pair + lane_half, both, 0.0).astype(BF16)
        for pair in range(n // 2)
    ]
    delta = jnp.dot(jnp.concatenate(masked, axis=1), up[...], preferred_element_type=F32)
    query = query + ADAPTER_SCALE * delta
    for step in range(2):
        for head in range(heads):
            pair_rows[pl.ds(step * heads + head, n, stride=16), :] = query[
                step * n : (step + 1) * n, head * HEAD_SIZE : (head + 1) * HEAD_SIZE
            ]
    for request in range(n):
        pair_send[request] = pair_rows[request * 16 : (request + 1) * 16, :].astype(BF16)

    def pair_copy(k, target):
        return pltpu.make_async_remote_copy(
            src_ref=pair_send.at[target],
            dst_ref=pair_received.at[me],
            send_sem=pair_send_sem.at[k],
            recv_sem=pair_sem.at[me],
            device_id={"adapter": target},
            device_id_type=MESH,
        )

    for mask in reversed(range(1, n)):
        pair_copy(mask, partner(mask)).start()
    pair_received[me] = pair_send[me]

    copies[4].wait()
    copies[5].wait()

    def finish_ranks(k, carry):
        rank_copy(k, sibling).wait_send()
        return carry

    lax.fori_loop(1, n, finish_ranks, 0)

    for k in [across, far + across, far]:
        own_copy(k, sibling).wait_send()
    for k in passed_on:
        across_copy(k).wait_send()

    def finish_forward(k, carry):
        sibling_copy(2 * k + core).wait_send()
        return carry

    lax.fori_loop(0, chips, finish_forward, 0)

    def pair_arrival(k, carry):
        source = lax.rem(me + n - k, n)
        pltpu.make_async_remote_copy(
            src_ref=pair_send.at[source],
            dst_ref=pair_received.at[source],
            send_sem=pair_send_sem.at[0],
            recv_sem=pair_sem.at[source],
            device_id={"adapter": source},
            device_id_type=MESH,
        ).wait_recv()
        return carry

    lax.fori_loop(1, n, pair_arrival, 0)

    columns = lax.broadcasted_iota(jnp.int32, (16, total), 1)
    steps = (lax.broadcasted_iota(jnp.int32, (16, total), 0) // heads) % 2
    valid = (columns < length) | ((columns >= capacity) & (columns - capacity <= steps))
    fresh = lax.broadcasted_iota(jnp.int32, (8, HEAD_SIZE), 0) < 2
    padding = jnp.zeros((8, HEAD_SIZE), F32)
    turned_queries = []
    for group in range(KEY_VALUE_HEADS):
        turned_query = jnp.concatenate(
            [
                pair_received[2 * group].astype(F32)[:8],
                pair_received[2 * group + 1].astype(F32)[:8],
            ],
            axis=0,
        )
        turned_query = turned_query * cosine[:16] + pltpu.roll(turned_query, half, 1) * sine[:16]
        turned_queries.append(turned_query.astype(BF16))
    new_keys = []
    new_values = []
    for group in range(KEY_VALUE_HEADS):
        key = pair_received[group].astype(F32)[8:]
        key = key * cosine[16:] + pltpu.roll(key, half, 1) * sine[16:]
        key = jnp.concatenate([jnp.where(fresh, key, 0.0), padding], axis=0)
        new_keys.append(key.astype(BF16))
        value = pair_received[KEY_VALUE_HEADS + group].astype(F32)[8:]
        value = jnp.concatenate([jnp.where(fresh, value, 0.0), padding], axis=0)
        new_values.append(value.astype(BF16))
    keys[capacity : capacity + 16, :] = jnp.concatenate(new_keys, axis=1)
    values[capacity : capacity + 16, :] = jnp.concatenate(new_values, axis=1)
    scores = [
        lax.dot_general(
            turned_queries[group],
            keys[:, group * HEAD_SIZE : (group + 1) * HEAD_SIZE],
            (((1,), (1,)), ((), ())),
            preferred_element_type=F32,
        )
        for group in range(KEY_VALUE_HEADS)
    ]
    scores = [jnp.where(valid, part * HEAD_SIZE ** (-0.5), -1e30) for part in scores]
    tops = [jnp.max(part, axis=1, keepdims=True) for part in scores]
    weights = [
        jnp.where(valid, jnp.exp(part - top), 0.0) for part, top in zip(scores, tops)
    ]
    sums = [jnp.sum(part, axis=1, keepdims=True) for part in weights]
    weights = [(part / whole).astype(BF16) for part, whole in zip(weights, sums)]
    mixed = [
        jnp.dot(
            weights[group],
            values[:, group * HEAD_SIZE : (group + 1) * HEAD_SIZE],
            preferred_element_type=F32,
        )
        for group in range(KEY_VALUE_HEADS)
    ]
    for group in range(KEY_VALUE_HEADS):
        for side in range(2):
            for step in range(2):
                for head in range(heads):
                    start = ((2 * group + side) * heads + head) * HEAD_SIZE
                    line = (side * 2 + step) * heads + head
                    result[step : step + 1, start : start + HEAD_SIZE] = mixed[group][
                        line : line + 1
                    ]
    out_ref[...] = result[...].astype(BF16)

    def finish(k, carry):
        pair_copy(k, sibling).wait_send()
        return carry

    lax.fori_loop(1, n, finish, 0)


def whole_block(
    hidden,
    input_norm_gain,
    query_weight,
    key_value_weight,
    adapter_down_weight,
    adapter_up_weight,
    key_value_cache,
    valid_cache_lengths,
    request_per_slot,
    slot_per_request,
):
    n = request_per_slot.shape[0]
    width = hidden.shape[2]
    blocks = width // HEAD_SIZE
    capacity = key_value_cache.shape[2]
    kv_width = key_value_cache.shape[3]
    total = capacity + HEAD_SIZE
    columns = query_weight.shape[1]
    in_hbm = pl.BlockSpec(memory_space=pltpu.HBM)
    in_vmem = pl.BlockSpec(memory_space=pltpu.VMEM)
    dma = pltpu.SemaphoreType.DMA
    call = pl.pallas_call(
        functools.partial(block_kernel, n, capacity),
        out_shape=jax.ShapeDtypeStruct((2, width), BF16),
        in_specs=[in_hbm] * 10,
        out_specs=in_vmem,
        scratch_shapes=[
            pltpu.SMEM(valid_cache_lengths.shape, jnp.int32),
            pltpu.SMEM(request_per_slot.shape[::-1], jnp.int32),
            pltpu.SMEM(slot_per_request.shape, jnp.int32),
            pltpu.VMEM((2, width), BF16),
            pltpu.VMEM((blocks, HEAD_SIZE), F32),
            pltpu.VMEM((width, columns), BF16),
            pltpu.VMEM((width, HEAD_SIZE), BF16),
            pltpu.VMEM((ADAPTER_RANK, width), BF16),
            pltpu.VMEM((n * ADAPTER_RANK, columns), BF16),
            pltpu.VMEM((total, kv_width), BF16),
            pltpu.VMEM((total, kv_width), BF16),
            pltpu.VMEM((n, 2 * blocks, HEAD_SIZE), BF16),
            pltpu.VMEM((2 * blocks * n, HEAD_SIZE), F32),
            pltpu.VMEM((2 * n, width), BF16),
            pltpu.VMEM((2 * blocks, HEAD_SIZE), F32),
            pltpu.VMEM((n, n, HEAD_SIZE), BF16),
            pltpu.VMEM((n * 16, HEAD_SIZE), F32),
            pltpu.VMEM((n, 16, HEAD_SIZE), BF16),
            pltpu.VMEM((n, 16, HEAD_SIZE), BF16),
            pltpu.VMEM((2, width), F32),
            dma((11,)),
            dma((n // 2,)),
            dma((n,)),
            dma((n // 2,)),
            dma((n,)),
            dma((n,)),
            dma((n,)),
            dma((n,)),
        ],
        compiler_params=pltpu.CompilerParams(
            collective_id=0, has_side_effects=True, vmem_limit_bytes=63 * 2 ** 20
        ),
        name="decode_block",
    )
    out = call(
        hidden.reshape(2, width),
        input_norm_gain.reshape(blocks, HEAD_SIZE),
        query_weight,
        key_value_weight,
        adapter_down_weight.reshape(ADAPTER_RANK, width),
        adapter_up_weight.reshape(n * ADAPTER_RANK, columns),
        key_value_cache,
        valid_cache_lengths,
        request_per_slot.T,
        slot_per_request,
    )
    return out.reshape(2, 1, width)


def on_device(*arguments):
    hidden, _, query_weight, key_value_weight, _, _, _, _, request_per_slot, _ = arguments
    fits = (
        hidden.shape[1] == 1
        and key_value_weight.shape[1] == HEAD_SIZE
        and query_weight.shape[1] == 4 * HEAD_SIZE
        and request_per_slot.shape[0] == 16
    )
    return whole_block(*arguments) if fits else with_collectives(*arguments)


def solution(mesh):
    in_specs = (
        P(None, ("replica", "adapter"), None),
        P(),
        P(None, "adapter"),
        P(None, "adapter"),
        P(("replica", "adapter"), None, None),
        P("replica", None, "adapter"),
        P(("replica", "adapter"), None, None, None),
        P(("replica", "adapter")),
        P("replica", None),
        P("replica"),
    )
    out_specs = P(None, ("replica", "adapter"), None)
    return jax.shard_map(
        on_device, mesh=mesh, in_specs=in_specs, out_specs=out_specs, check_vma=False
    )
```
